32 devices in a mesh: req: 8 (over z, y), tp: 4 (over x, core).
Axes of the slice: x: 2, y: 2, z: 4, core: 2. Of those that a mesh axis runs over, the one named last changes fastest.
Arguments:
- tokens: bfloat16 [3072, 3200], P('req'), may hold values from -6 to 6
- norm_gain: float32 [3200], replicated, may hold values from 0.5 to 2
- w_qkv: bfloat16 [3200, 6144], P('req', 'tp'), may hold values from -1 to 1
- q_gain: float32 [2048], P('tp'), may hold values from 0.5 to 2.5
- k_gain: float32 [2048], P('tp'), may hold values from 0.5 to 2.5
- w_out: bfloat16 [2048, 3200], P('tp', 'req'), may hold values from -0.125 to 0.125
- grids: int32 [24, 2], P('req'), may hold values from 2 to 16, as said below
- owners: int32 [768], P('req'), may hold values from 0 to 7, as said below
- proj_gain: float32 [4, 3200], P(None, 'tp'), may hold values from 0.5 to 2
- proj_bias: float32 [4, 3200], P(None, 'tp'), may hold values from -3 to 3
Outputs:
- received: bfloat16 [1536, 4, 3200], P('req', None, 'tp')
The draws below stay inside these ranges and needn't reach their ends.
Inputs may be any that keep to these rules, and one draw needn't show every extreme that they name: `grids`: each image spans at least 2 half grid rows. The images of one device together take at most 96 merged slots, and on one device in every draw exactly 96. `owners`: no device's merged slots, live or padding, name one owner more than 24 times; in every draw one owner is named exactly 24 times by every device.
All inputs are finite; a program needn't handle non-finite values.
Results may differ from the reference program's by a relative error of at most 0.009.
Values may be sent and summed in bfloat16 or wider, within the bound.
No kernel may reach another device: no remote copies, remote signals or barrier semaphores. Data moves between devices by JAX's collectives and lax.ppermute only.
A program may use at most 128 MiB of HBM per device.

```python
import math
import jax
import jax.numpy as jnp
from jax import lax

D = 3200
HEADS = 16
HEAD_DIM = 128
IMG_DEV = 3
TOK_DEV = 384
MRG_DEV = 96
CAP = 24
TOKENS = 3072
N_REQ = 8
N_TP = 4


def draw_tokens(key, part):
    values = jnp.clip(jax.random.normal(jax.random.fold_in(key, 1), (TOKENS, D), jnp.float32), -6.0, 6.0)
    return values.astype(jnp.bfloat16)


def draw_w_qkv(key, part):
    scale = 1.0 / math.sqrt(D)
    values = jnp.clip(jax.random.normal(jax.random.fold_in(key, 3), (D, HEADS, 3, HEAD_DIM), jnp.float32), -6.0, 6.0) * scale
    return jnp.clip(values, -1.0, 1.0).reshape(D, 3 * HEADS * HEAD_DIM).astype(jnp.bfloat16)


def draw_grids(key, part):
    device_count = TOKENS // TOK_DEV
    third = MRG_DEV // 3
    key_rows, key_cols, key_full = jax.random.split(key, 3)
    half_rows = 2 * jax.random.randint(key_rows, (device_count, 3), 1, 3)
    widest = third // half_rows
    half_cols = jnp.maximum(widest - jax.random.randint(key_cols, (device_count, 3), 0, 2), 1)
    full_device = jax.random.randint(key_full, (), 0, device_count)
    chosen = jnp.arange(device_count) == full_device
    full_rows = jnp.array([2, 2, 4], jnp.int32)
    full_cols = jnp.array([MRG_DEV // 6, MRG_DEV // 6, MRG_DEV // 12], jnp.int32)
    half_rows = jnp.where(chosen[:, None], full_rows[None, :], half_rows)
    half_cols = jnp.where(chosen[:, None], full_cols[None, :], half_cols)
    return jnp.stack([half_rows, half_cols], axis=-1).reshape(device_count * 3, 2).astype(jnp.int32)


def draw_owners(key, part):
    device_count = TOKENS // TOK_DEV
    key_full, key_rest = jax.random.split(key)
    full_owner = jax.random.randint(key_full, (), 0, device_count)
    source_keys = jax.random.split(key_rest, device_count)

    def one_source(source_key):
        picked = jax.random.permutation(source_key, (device_count - 1) * CAP)[:MRG_DEV - CAP]
        shifted = picked + CAP * (picked // CAP >= full_owner).astype(picked.dtype)
        head_part = jnp.full((CAP,), full_owner, dtype=picked.dtype)
        return jnp.concatenate([head_part, shifted // CAP])
    return jax.vmap(one_source)(source_keys).reshape(-1).astype(jnp.int32)


def shard_levels(rng, extent, pieces, smallest, top_value):
    def one(axis_at, blocks):
        heights = jax.random.uniform(jax.random.fold_in(jax.random.fold_in(rng, 6), axis_at), (blocks,), jnp.float32, smallest / len(pieces), top_value / len(pieces))
        return jnp.repeat(jnp.exp(heights), extent[axis_at] // blocks).reshape((-1,) + (1,) * (len(extent) - axis_at - 1))

    gain = one(*pieces[0])
    for cut in pieces[1:]:
        gain = gain * one(*cut)
    return gain


def noise(key, extent, scale, most, cuts=(), held_as=jnp.bfloat16):
    values = scale * jax.random.normal(key, extent, jnp.float32)
    if cuts:
        values = values * shard_levels(key, extent, cuts, -0.22, 0.18)
    return jnp.clip(values, -most, most).astype(held_as)


def setup_inputs(seed: int = 0) -> dict:
    arg_keys = jax.random.split(jax.random.key(seed), 11)
    return {
        "tokens": draw_tokens(jax.random.fold_in(arg_keys[10], 71), 0),
        "norm_gain": jnp.clip(jnp.exp(jax.random.uniform(arg_keys[1], (D,), jnp.float32, math.log(0.5), math.log(2.0))), 0.5, 2.0),
        "w_qkv": draw_w_qkv(jax.random.fold_in(arg_keys[10], 71), 0),
        "q_gain": jnp.clip(jnp.exp(math.log(2.5) - 1.609438 * jax.random.uniform(arg_keys[3], (HEADS * HEAD_DIM,), jnp.float32) ** shard_levels(arg_keys[3], (HEADS * HEAD_DIM,), ((0, 4),), -0.2, 0.2)), 0.5, 2.5),
        "k_gain": jnp.clip(jnp.exp(math.log(2.5) - 1.609438 * jax.random.uniform(arg_keys[4], (HEADS * HEAD_DIM,), jnp.float32) ** shard_levels(arg_keys[4], (HEADS * HEAD_DIM,), ((0, 4),), -0.2, 0.2)), 0.5, 2.5),
        "w_out": noise(arg_keys[5], (HEADS * HEAD_DIM, D), (HEADS * HEAD_DIM) ** -0.5, 0.125, ((0, 4), (1, 8))),
        "grids": draw_grids(jax.random.fold_in(arg_keys[10], 71), 0),
        "owners": draw_owners(jax.random.fold_in(arg_keys[10], 71), 0),
        "proj_gain": jnp.clip(jnp.exp(math.log(2.0) - 1.3862944 * jax.random.uniform(arg_keys[8], (4, D), jnp.float32) ** shard_levels(arg_keys[8], (4, D), ((1, 4),), -0.2, 0.2)), 0.5, 2.0),
        "proj_bias": noise(arg_keys[9], (4, D), 0.5, 3.0, ((1, 4),), jnp.float32),
    }


def merge_layout(grid, token_count, slot_count):
    half_rows = grid[:, 0]
    half_cols = grid[:, 1]
    image_slots = half_rows * half_cols
    slot_ends = jnp.cumsum(image_slots).astype(jnp.int32)
    slot_starts = slot_ends - image_slots
    slot_ids = jnp.arange(slot_count, dtype=jnp.int32)
    image_ids = lax.optimization_barrier(jnp.sum((slot_ids[:, None] >= slot_ends[None, :]).astype(jnp.int32), axis=1)).astype(jnp.int32)
    image_count = grid.shape[0]
    is_live = image_ids < image_count
    one_hot = (image_ids[:, None] == jnp.arange(image_count, dtype=jnp.int32)[None, :]).astype(jnp.int32)
    cols_here = jnp.maximum(lax.optimization_barrier(jnp.sum(one_hot * half_cols[None, :], axis=1)), 1).astype(jnp.int32)
    start_here = lax.optimization_barrier(jnp.sum(one_hot * slot_starts[None, :], axis=1)).astype(jnp.int32)
    offset = slot_ids - start_here
    row_half = offset // cols_here
    col_half = offset % cols_here
    first_row = 4 * start_here + 4 * row_half * cols_here + 2 * col_half
    patch_rows = jnp.stack([first_row, first_row + 1, first_row + 2 * cols_here, first_row + 2 * cols_here + 1], axis=1)
    patch_rows = jnp.where(is_live[:, None], patch_rows, 0).astype(jnp.int32)
    token_ids = jnp.arange(token_count, dtype=jnp.int32)
    segment = lax.optimization_barrier(jnp.sum((token_ids[:, None] >= 4 * slot_ends[None, :]).astype(jnp.int32), axis=1)).astype(jnp.int32)
    return (patch_rows, is_live, segment)

def owner_ranks(owner_ids, is_live):
    slot_ids = jnp.arange(owner_ids.shape[0], dtype=jnp.int32)
    earlier = (owner_ids[:, None] == owner_ids[None, :]) & (slot_ids[None, :] < slot_ids[:, None]) & is_live[None, :]
    return lax.optimization_barrier(jnp.sum(earlier.astype(jnp.int32), axis=1)).astype(jnp.int32)

def reference(tokens, norm_gain, w_qkv, q_gain, k_gain, w_out, grids, owners, proj_gain, proj_bias):
    head_width = HEADS * HEAD_DIM
    head_share = head_width // N_TP
    score_scale = 1.0 / math.sqrt(HEAD_DIM)

    def one_device(device):
        token_rows = lax.dynamic_slice_in_dim(tokens, device * TOK_DEV, TOK_DEV, 0)
        grid = lax.dynamic_slice_in_dim(grids, device * IMG_DEV, IMG_DEV, 0)
        owner_ids = lax.dynamic_slice_in_dim(owners, device * MRG_DEV, MRG_DEV, 0)
        patch_rows, is_live, segment = merge_layout(grid, TOK_DEV, MRG_DEV)
        token_float = token_rows.astype(jnp.float32)
        mean_square = lax.optimization_barrier(jnp.mean(token_float * token_float, axis=1, keepdims=True))
        normed = (token_float * lax.rsqrt(mean_square + 1e-06) * norm_gain).astype(jnp.bfloat16)
        projected = jnp.dot(normed, w_qkv, preferred_element_type=jnp.float32).reshape(TOK_DEV, HEADS, 3, HEAD_DIM)
        queries = projected[:, :, 0]
        key_vecs = projected[:, :, 1]
        values = projected[:, :, 2].astype(jnp.bfloat16)
        q_scale = lax.rsqrt(lax.optimization_barrier(jnp.sum(queries * queries, axis=(1, 2))) / head_width + 1e-06)
        k_scale = lax.rsqrt(lax.optimization_barrier(jnp.sum(key_vecs * key_vecs, axis=(1, 2))) / head_width + 1e-06)
        q_normed = queries * q_scale[:, None, None] * q_gain.reshape(HEADS, HEAD_DIM)
        k_normed = key_vecs * k_scale[:, None, None] * k_gain.reshape(HEADS, HEAD_DIM)
        scores = jnp.einsum('qhd,khd->hqk', q_normed, k_normed, precision=lax.Precision.HIGHEST) * score_scale
        same_image = segment[:, None] == segment[None, :]
        scores = jnp.where(same_image[None], scores, -1e+30)
        row_top = lax.optimization_barrier(jnp.max(scores, axis=2, keepdims=True))
        weights_raw = jnp.exp(scores - row_top)
        probs = (weights_raw / lax.optimization_barrier(jnp.sum(weights_raw, axis=2, keepdims=True))).astype(jnp.bfloat16)
        attended = jnp.einsum('hqk,khd->qhd', probs.astype(jnp.float32), values.astype(jnp.float32))
        attended = attended.astype(jnp.bfloat16).reshape(TOK_DEV, head_width)
        summed = jnp.zeros((TOK_DEV, D), jnp.float32)
        for group in range(N_TP):
            lower = group * head_share
            partial_term = jnp.dot(attended[:, lower:lower + head_share], w_out[lower:lower + head_share], preferred_element_type=jnp.float32).astype(jnp.bfloat16)
            partial_term = lax.optimization_barrier(partial_term)
            summed = summed + partial_term.astype(jnp.float32)
        hidden = (token_float + summed).astype(jnp.bfloat16)
        merged = hidden[patch_rows].astype(jnp.float32)
        merged = jnp.where(is_live[:, None, None], merged, 0.0)
        feature_total = 4 * D
        mean_value = lax.optimization_barrier(jnp.sum(merged, axis=(1, 2))) / feature_total
        mean_sq = lax.optimization_barrier(jnp.sum(merged * merged, axis=(1, 2))) / feature_total
        variance = mean_sq - mean_value * mean_value
        normed_rows = (merged - mean_value[:, None, None]) * lax.rsqrt(variance + 1e-05)[:, None, None] * proj_gain + proj_bias
        normed_rows = jnp.where(is_live[:, None, None], normed_rows, 0.0).astype(jnp.bfloat16)
        ranks = owner_ranks(owner_ids, is_live)
        return (normed_rows, is_live, ranks, owner_ids)
    rows_all, live_all, rank_all, owner_all = lax.map(one_device, jnp.arange(N_REQ, dtype=jnp.int32))
    slot_total = N_REQ * N_REQ * CAP
    sources = jnp.arange(N_REQ, dtype=jnp.int32)[:, None]
    target = owner_all * (N_REQ * CAP) + sources * CAP + rank_all
    target = jnp.where(live_all, target, slot_total).astype(jnp.int32)
    result = jnp.zeros((slot_total, 4, D), jnp.bfloat16)
    result = result.at[target.reshape(-1)].set(rows_all.reshape(-1, 4, D), mode='drop')
    return result
```

```python
import math

import jax
import jax.numpy as jnp
from jax import lax
from jax.sharding import PartitionSpec as P

D = 3200
HEADS = 16
HEAD_DIM = 128
BF16 = jnp.bfloat16
F32 = jnp.float32


def merge_layout(grid, token_count, slot_count):
    half_rows = grid[:, 0]
    half_cols = grid[:, 1]
    image_slots = half_rows * half_cols
    slot_ends = jnp.cumsum(image_slots)
    slot_starts = slot_ends - image_slots
    slot_ids = jnp.arange(slot_count, dtype=jnp.int32)
    image_ids = jnp.sum((slot_ids[:, None] >= slot_ends[None, :]).astype(jnp.int32), axis=1)
    image_count = grid.shape[0]
    is_live = image_ids < image_count
    one_hot = (image_ids[:, None] == jnp.arange(image_count, dtype=jnp.int32)[None, :]).astype(
        jnp.int32
    )
    cols_here = jnp.maximum(jnp.sum(one_hot * half_cols[None, :], axis=1), 1)
    start_here = jnp.sum(one_hot * slot_starts[None, :], axis=1)
    offset = slot_ids - start_here
    row_half = offset // cols_here
    col_half = offset % cols_here
    first_row = 4 * start_here + 4 * row_half * cols_here + 2 * col_half
    patch_rows = jnp.stack(
        [first_row, first_row + 1, first_row + 2 * cols_here, first_row + 2 * cols_here + 1], axis=1
    )
    patch_rows = jnp.where(is_live[:, None], patch_rows, 0)
    token_ids = jnp.arange(token_count, dtype=jnp.int32)
    segment = jnp.sum((token_ids[:, None] >= 4 * slot_ends[None, :]).astype(jnp.int32), axis=1)
    return (patch_rows, is_live, segment)


def owner_ranks(owner_ids, is_live):
    slot_ids = jnp.arange(owner_ids.shape[0], dtype=jnp.int32)
    earlier = (
        (owner_ids[:, None] == owner_ids[None, :])
        & (slot_ids[None, :] < slot_ids[:, None])
        & is_live[None, :]
    )
    return jnp.sum(earlier.astype(jnp.int32), axis=1)


def dest_tokens(patch_rows, is_live, owners, capacity, devices_req):
    ranks = owner_ranks(owners, is_live)
    target = jnp.where(is_live, owners * capacity + ranks, -1)
    rows = jnp.arange(devices_req * capacity, dtype=jnp.int32)
    hit = (target[None, :] == rows[:, None]).astype(jnp.int32)
    return jnp.sum(hit[:, :, None] * (patch_rows[None] + 1), axis=1) - 1


def swap(value, axis, bit):
    count = lax.axis_size(axis)
    return lax.ppermute(value, axis, [(i, i ^ bit) for i in range(count)])


def ring(value):
    count = lax.axis_size("req")
    return lax.ppermute(value, "req", [(i, (i + 2) % count) for i in range(count)])


def after(value, *first):
    return lax.optimization_barrier((value,) + first)[0]


def body(tokens, norm_gain, w_qkv, q_gain, k_gain, w_out, grids, owners, proj_gain, proj_bias):
    token_count = tokens.shape[0]
    slot_count = owners.shape[0]
    quarter = proj_gain.shape[1]
    head_share = q_gain.shape[0]
    head_count = head_share // HEAD_DIM
    head_width = HEADS * HEAD_DIM
    score_scale = 1.0 / math.sqrt(HEAD_DIM)
    feature_total = 4 * D
    devices_req = lax.axis_size("req")
    devices_tp = lax.axis_size("tp")
    depth = w_qkv.shape[0]
    planes = devices_req // 2
    use_ring = planes == devices_tp
    capacity = max(2, (2 * slot_count + devices_req - 1) // devices_req)
    me = lax.axis_index("req")
    plane, side = me // 2, me % 2
    column = lax.axis_index("tp")

    w_parts = w_qkv.reshape(depth, head_count, 3, HEAD_DIM)
    w_q, w_k, w_v = (w_parts[:, :, i].reshape(depth, head_share) for i in range(3))
    w_o = w_out.T
    if use_ring:
        q_blocks, k_blocks, v_blocks, o_blocks = [w_q], [w_k], [w_v], [w_o]
        for step in range(1, planes):
            q_blocks.append(ring(q_blocks[-1]))
            k_blocks.append(ring(k_blocks[-1]))
        v_blocks[0] = after(w_v, q_blocks[2])
        o_blocks[0] = after(w_o, k_blocks[2])
        for step in range(1, planes):
            v_blocks.append(ring(v_blocks[-1]))
            o_blocks.append(ring(o_blocks[-1]))

    patch_rows, is_live, segment = merge_layout(grids, token_count, slot_count)
    row_tokens = dest_tokens(patch_rows, is_live, owners, capacity, devices_req)
    token_float = tokens.astype(F32)
    mean_square = jnp.mean(token_float * token_float, axis=1, keepdims=True)
    normed = (token_float * lax.rsqrt(mean_square + 1e-06) * norm_gain).astype(BF16)

    by_side = normed.reshape(token_count, planes, 2, depth)
    mine = lax.dynamic_index_in_dim(by_side, side, 2, keepdims=False)
    others = lax.dynamic_index_in_dim(by_side, 1 - side, 2, keepdims=False)
    theirs = swap(others.reshape(token_count, planes * depth), "req", 1)
    both = jnp.concatenate([mine.reshape(token_count, planes * depth), theirs], axis=0)

    if use_ring:
        both_blocks = both.reshape(2 * token_count, planes, depth).transpose(1, 0, 2)

        def project(blocks):
            total = None
            for step, block in enumerate(blocks):
                rows = lax.dynamic_index_in_dim(
                    both_blocks, (plane + planes - step) % planes, 0, keepdims=False
                )
                term = jnp.dot(rows, block, preferred_element_type=F32)
                total = term if total is None else total + term
            return total
    else:
        groups = [list(range(i, devices_req, 2)) for i in range(2)]

        def project(block):
            whole = lax.all_gather(block, "req", axis=0, tiled=True, axis_index_groups=groups)
            return jnp.dot(both, whole, preferred_element_type=F32)

        q_blocks, k_blocks, v_blocks = w_q, w_k, w_v

    def projected(blocks):
        total = project(blocks)
        return total[:token_count] + swap(total[token_count:].astype(BF16), "req", 1).astype(F32)

    queries = projected(q_blocks)
    key_vecs = projected(k_blocks)
    values = projected(v_blocks).astype(BF16).reshape(token_count, head_count, HEAD_DIM)
    local_q = jnp.sum(queries * queries, axis=1)
    local_k = jnp.sum(key_vecs * key_vecs, axis=1)
    q_total, k_total = lax.psum((local_q, local_k), "tp")
    q_scale = lax.rsqrt(q_total / head_width + 1e-06)
    k_scale = lax.rsqrt(k_total / head_width + 1e-06)
    q_normed = (queries * q_scale[:, None] * q_gain).reshape(token_count, head_count, HEAD_DIM)
    k_normed = (key_vecs * k_scale[:, None] * k_gain).reshape(token_count, head_count, HEAD_DIM)
    scores = (
        jnp.einsum("qhd,khd->hqk", q_normed, k_normed, precision=lax.Precision.HIGHEST)
        * score_scale
    )
    same_image = segment[:, None] == segment[None, :]
    scores = jnp.where(same_image[None], scores, -1e30)
    row_top = jnp.max(scores, axis=2, keepdims=True)
    weights_raw = jnp.exp(scores - row_top)
    probs = (weights_raw / jnp.sum(weights_raw, axis=2, keepdims=True)).astype(BF16)
    attended = jnp.einsum("hqk,khd->qhd", probs, values, preferred_element_type=F32)
    attended = attended.astype(BF16).reshape(token_count, head_share)

    contract_last = (((1,), (1,)), ((), ()))
    if use_ring:
        terms = []
        for block in o_blocks:
            peer = swap(block, "req", 1)
            low = jnp.where(side == 0, block, peer)
            high = jnp.where(side == 0, peer, block)
            pair = jnp.concatenate([low, high], axis=0)
            terms.append(
                lax.dot_general(attended, pair, contract_last, preferred_element_type=F32)
            )
        terms = jnp.stack(terms).astype(BF16)

        def term_of(index):
            return lax.dynamic_index_in_dim(
                terms, (plane + planes - index) % planes, 0, keepdims=False
            )
    else:
        whole = lax.all_gather(w_o, "req", axis=0, tiled=True)
        terms = lax.dot_general(attended, whole, contract_last, preferred_element_type=F32)
        terms = terms.astype(BF16).reshape(token_count, devices_tp, quarter).transpose(1, 0, 2)

        def term_of(index):
            return lax.dynamic_index_in_dim(terms, index, 0, keepdims=False)

    far = column ^ 2
    sent = jnp.stack([term_of(column ^ 1), term_of(far ^ 1)])
    got = swap(sent, "tp", 1).astype(F32)
    mine_near = term_of(column).astype(F32) + got[0]
    mine_far = term_of(far).astype(F32) + got[1]
    attn_out = mine_near + swap(mine_far.astype(BF16), "tp", 2).astype(F32)

    token_mine = lax.dynamic_slice_in_dim(tokens, column * quarter, quarter, 1).astype(F32)
    hidden = (token_mine + attn_out).astype(BF16)

    token_ids = jnp.arange(token_count, dtype=jnp.int32)
    chosen = row_tokens.reshape(-1)[:, None] == token_ids[None, :]
    packed = jnp.dot(chosen.astype(BF16), hidden, preferred_element_type=F32).astype(BF16)
    packed = packed.reshape(devices_req, capacity * 4, quarter)
    arrived = lax.all_to_all(packed, "req", split_axis=0, concat_axis=0, tiled=True)

    hidden_float = hidden.astype(F32)
    token_sums = jnp.stack(
        [jnp.sum(hidden_float, axis=1), jnp.sum(hidden_float * hidden_float, axis=1)]
    )
    token_sums = lax.psum(token_sums, "tp")
    in_row = jnp.any(row_tokens[:, :, None] == token_ids[None, None, :], axis=1)
    row_sums = jnp.sum(jnp.where(in_row[None], token_sums[:, None, :], 0.0), axis=2)
    mean_value = row_sums[0] / feature_total
    variance = row_sums[1] / feature_total - mean_value * mean_value
    row_live = (row_tokens[:, 0] >= 0).astype(F32)
    inverse = lax.rsqrt(variance + 1e-05) * row_live
    stats = jnp.stack([inverse, -mean_value * inverse, row_live]).reshape(3, devices_req, capacity)
    stats = lax.all_to_all(stats, "req", split_axis=1, concat_axis=1, tiled=True)
    stats = stats.reshape(3, devices_req * capacity, 1, 1)

    arrived = arrived.reshape(devices_req * capacity, 4, quarter).astype(F32)
    result = (arrived * stats[0] + stats[1]) * proj_gain + stats[2] * proj_bias
    return result.astype(BF16)


def solution(mesh):
    placed = (
        P("req", None),
        P(),
        P("req", "tp"),
        P("tp"),
        P("tp"),
        P("tp", "req"),
        P("req", None),
        P("req"),
        P(None, "tp"),
        P(None, "tp"),
    )
    return jax.shard_map(
        body, mesh=mesh, in_specs=placed, out_specs=P("req", None, "tp"), check_vma=False
    )
```

```python
import math

import jax
import jax.numpy as jnp
from jax import lax
from jax.experimental import pallas as pl
from jax.experimental.pallas import tpu as pltpu
from jax.sharding import PartitionSpec as P

D = 3200
HEADS = 16
HEAD_DIM = 128
BF16 = jnp.bfloat16
F32 = jnp.float32


def merge_layout(grid, token_count, slot_count):
    half_rows = grid[:, 0]
    half_cols = grid[:, 1]
    image_slots = half_rows * half_cols
    slot_ends = jnp.cumsum(image_slots)
    slot_starts = slot_ends - image_slots
    slot_ids = jnp.arange(slot_count, dtype=jnp.int32)
    image_ids = jnp.sum((slot_ids[:, None] >= slot_ends[None, :]).astype(jnp.int32), axis=1)
    image_count = grid.shape[0]
    is_live = image_ids < image_count
    one_hot = (image_ids[:, None] == jnp.arange(image_count, dtype=jnp.int32)[None, :]).astype(
        jnp.int32
    )
    cols_here = jnp.maximum(jnp.sum(one_hot * half_cols[None, :], axis=1), 1)
    start_here = jnp.sum(one_hot * slot_starts[None, :], axis=1)
    offset = slot_ids - start_here
    row_half = offset // cols_here
    col_half = offset % cols_here
    first_row = 4 * start_here + 4 * row_half * cols_here + 2 * col_half
    patch_rows = jnp.stack(
        [first_row, first_row + 1, first_row + 2 * cols_here, first_row + 2 * cols_here + 1], axis=1
    )
    patch_rows = jnp.where(is_live[:, None], patch_rows, 0)
    token_ids = jnp.arange(token_count, dtype=jnp.int32)
    segment = jnp.sum((token_ids[:, None] >= 4 * slot_ends[None, :]).astype(jnp.int32), axis=1)
    return (patch_rows, is_live, segment)


def owner_ranks(owner_ids, is_live):
    slot_ids = jnp.arange(owner_ids.shape[0], dtype=jnp.int32)
    earlier = (
        (owner_ids[:, None] == owner_ids[None, :])
        & (slot_ids[None, :] < slot_ids[:, None])
        & is_live[None, :]
    )
    return jnp.sum(earlier.astype(jnp.int32), axis=1)


def dest_tokens(patch_rows, is_live, owners, capacity, devices_req):
    ranks = owner_ranks(owners, is_live)
    target = jnp.where(is_live, owners * capacity + ranks, -1)
    rows = jnp.arange(devices_req * capacity, dtype=jnp.int32)
    hit = (target[None, :] == rows[:, None]).astype(jnp.int32)
    return jnp.sum(hit[:, :, None] * (patch_rows[None] + 1), axis=1) - 1


def swap(value, axis, bit):
    count = lax.axis_size(axis)
    return lax.ppermute(value, axis, [(i, i ^ bit) for i in range(count)])


def ring(value):
    count = lax.axis_size("req")
    return lax.ppermute(value, "req", [(i, (i + 2) % count) for i in range(count)])


def split_kernel(w_ref, q_ref, k_ref, v_ref):
    for head in range(q_ref.shape[1] // HEAD_DIM):
        to = pl.ds(head * HEAD_DIM, HEAD_DIM)
        for i, ref in enumerate((q_ref, k_ref, v_ref)):
            ref[:, to] = w_ref[:, pl.ds((3 * head + i) * HEAD_DIM, HEAD_DIM)]


def split_heads(w_qkv):
    depth, columns = w_qkv.shape
    part = jax.ShapeDtypeStruct((depth, columns // 3), w_qkv.dtype)
    return pl.pallas_call(
        split_kernel,
        out_shape=(part,) * 3,
        in_specs=[pl.BlockSpec(memory_space=pltpu.VMEM)],
        out_specs=(pl.BlockSpec(memory_space=pltpu.VMEM),) * 3,
        compiler_params=pltpu.CompilerParams(vmem_limit_bytes=16 << 20),
        cost_estimate=pl.CostEstimate(
            flops=0, bytes_accessed=4 * depth * columns, transcendentals=0
        ),
        name="split_heads",
    )(w_qkv)


def scatter_rows(packed, me, by_permutes):
    if not by_permutes:
        return lax.all_to_all(packed, "req", split_axis=0, concat_axis=0, tiled=True)
    count = packed.shape[0]
    arrived = jnp.zeros_like(packed)
    for bits in range(count):
        block = lax.dynamic_index_in_dim(packed, me ^ bits, 0, keepdims=False)
        if bits:
            block = swap(block, "req", bits)
        arrived = lax.dynamic_update_index_in_dim(arrived, block, me ^ bits, 0)
    return arrived


def after(value, *first):
    return lax.optimization_barrier((value,) + first)[0]


def body(tokens, norm_gain, w_qkv, q_gain, k_gain, w_out, grids, owners, proj_gain, proj_bias):
    token_count = tokens.shape[0]
    slot_count = owners.shape[0]
    quarter = proj_gain.shape[1]
    head_share = q_gain.shape[0]
    head_count = head_share // HEAD_DIM
    head_width = HEADS * HEAD_DIM
    score_scale = 1.0 / math.sqrt(HEAD_DIM)
    feature_total = 4 * D
    devices_req = lax.axis_size("req")
    devices_tp = lax.axis_size("tp")
    depth = w_qkv.shape[0]
    planes = devices_req // 2
    use_ring = planes == devices_tp
    capacity = max(2, (2 * slot_count + devices_req - 1) // devices_req)
    me = lax.axis_index("req")
    plane, side = me // 2, me % 2
    column = lax.axis_index("tp")

    if depth % 16 == 0:
        w_q, w_k, w_v = split_heads(w_qkv)
    else:
        w_parts = w_qkv.reshape(depth, head_count, 3, HEAD_DIM)
        w_q, w_k, w_v = (w_parts[:, :, i].reshape(depth, head_share) for i in range(3))
    w_o = w_out.T
    if use_ring:
        q_blocks, k_blocks, v_blocks, o_blocks = [w_q], [w_k], [w_v], [w_o]
        for step in range(1, planes):
            q_blocks.append(ring(q_blocks[-1]))
            k_blocks.append(ring(k_blocks[-1]))
        v_blocks[0] = after(w_v, q_blocks[-1])
        o_blocks[0] = after(w_o, k_blocks[-1])
        for step in range(1, planes):
            v_blocks.append(ring(v_blocks[-1]))
            o_blocks.append(ring(o_blocks[-1]))

    patch_rows, is_live, segment = merge_layout(grids, token_count, slot_count)
    row_tokens = dest_tokens(patch_rows, is_live, owners, capacity, devices_req)
    token_float = tokens.astype(F32)
    mean_square = jnp.mean(token_float * token_float, axis=1, keepdims=True)
    normed = (token_float * lax.rsqrt(mean_square + 1e-06) * norm_gain).astype(BF16)

    by_side = normed.reshape(token_count, planes, 2, depth)
    mine = lax.dynamic_index_in_dim(by_side, side, 2, keepdims=False)
    others = lax.dynamic_index_in_dim(by_side, 1 - side, 2, keepdims=False)
    theirs = swap(others.reshape(token_count, planes * depth), "req", 1)
    both = jnp.concatenate([mine.reshape(token_count, planes * depth), theirs], axis=0)

    if use_ring:

        def project(blocks):
            whole = jnp.zeros((planes * depth, head_share), BF16)
            for step, block in enumerate(blocks):
                first_row = (plane + planes - step) % planes * depth
                whole = lax.dynamic_update_slice_in_dim(whole, block, first_row, 0)
            return jnp.dot(both, whole, preferred_element_type=F32)

    else:
        groups = [list(range(i, devices_req, 2)) for i in range(2)]

        def project(block):
            whole = lax.all_gather(block, "req", axis=0, tiled=True, axis_index_groups=groups)
            return jnp.dot(both, whole, preferred_element_type=F32)

        q_blocks, k_blocks, v_blocks = w_q, w_k, w_v

    def projected(blocks):
        total = project(blocks)
        return total[:token_count] + swap(total[token_count:].astype(BF16), "req", 1).astype(F32)

    queries = projected(q_blocks)
    key_vecs = projected(k_blocks)
    values = projected(v_blocks).astype(BF16).reshape(token_count, head_count, HEAD_DIM)
    local_q = jnp.sum(queries * queries, axis=1)
    local_k = jnp.sum(key_vecs * key_vecs, axis=1)
    q_total, k_total = lax.psum((local_q, local_k), "tp")
    q_scale = lax.rsqrt(q_total / head_width + 1e-06)
    k_scale = lax.rsqrt(k_total / head_width + 1e-06)
    q_normed = (queries * q_scale[:, None] * q_gain).reshape(token_count, head_count, HEAD_DIM)
    k_normed = (key_vecs * k_scale[:, None] * k_gain).reshape(token_count, head_count, HEAD_DIM)
    scores = (
        jnp.einsum("qhd,khd->hqk", q_normed, k_normed, precision=lax.Precision.HIGHEST)
        * score_scale
    )
    same_image = segment[:, None] == segment[None, :]
    scores = jnp.where(same_image[None], scores, -1e30)
    row_top = jnp.max(scores, axis=2, keepdims=True)
    weights_raw = jnp.exp(scores - row_top)
    probs = (weights_raw / jnp.sum(weights_raw, axis=2, keepdims=True)).astype(BF16)
    attended = jnp.einsum("hqk,khd->qhd", probs, values, preferred_element_type=F32)
    attended = attended.astype(BF16).reshape(token_count, head_share)

    contract_last = (((1,), (1,)), ((), ()))
    if use_ring:
        terms = []
        for block in o_blocks:
            peer = swap(block, "req", 1)
            low = jnp.where(side == 0, block, peer)
            high = jnp.where(side == 0, peer, block)
            pair = jnp.concatenate([low, high], axis=0)
            terms.append(
                lax.dot_general(attended, pair, contract_last, preferred_element_type=F32)
            )
        terms = jnp.stack(terms).astype(BF16)

        def term_of(index):
            return lax.dynamic_index_in_dim(
                terms, (plane + planes - index) % planes, 0, keepdims=False
            )
    else:
        whole = lax.all_gather(w_o, "req", axis=0, tiled=True)
        terms = lax.dot_general(attended, whole, contract_last, preferred_element_type=F32)
        terms = terms.astype(BF16).reshape(token_count, devices_tp, quarter).transpose(1, 0, 2)

        def term_of(index):
            return lax.dynamic_index_in_dim(terms, index, 0, keepdims=False)

    far = column ^ 2
    sent = jnp.stack([term_of(column ^ 1), term_of(far ^ 1)])
    got = swap(sent, "tp", 1).astype(F32)
    mine_near = term_of(column).astype(F32) + got[0]
    mine_far = term_of(far).astype(F32) + got[1]
    attn_out = mine_near + swap(mine_far.astype(BF16), "tp", 2).astype(F32)

    token_mine = lax.dynamic_slice_in_dim(tokens, column * quarter, quarter, 1).astype(F32)
    hidden = (token_mine + attn_out).astype(BF16)

    token_ids = jnp.arange(token_count, dtype=jnp.int32)
    chosen = row_tokens.reshape(-1)[:, None] == token_ids[None, :]
    packed = jnp.dot(chosen.astype(BF16), hidden, preferred_element_type=F32).astype(BF16)
    packed = packed.reshape(devices_req, capacity * 4, quarter)
    arrived = scatter_rows(packed, me, use_ring)

    hidden_float = hidden.astype(F32)
    token_sums = jnp.stack(
        [jnp.sum(hidden_float, axis=1), jnp.sum(hidden_float * hidden_float, axis=1)]
    )
    if use_ring:
        token_sums = token_sums + sum(swap(token_sums, "tp", bit) for bit in range(1, devices_tp))
    else:
        token_sums = lax.psum(token_sums, "tp")
    in_row = jnp.any(row_tokens[:, :, None] == token_ids[None, None, :], axis=1)
    row_sums = jnp.sum(jnp.where(in_row[None], token_sums[:, None, :], 0.0), axis=2)
    mean_value = row_sums[0] / feature_total
    variance = row_sums[1] / feature_total - mean_value * mean_value
    row_live = (row_tokens[:, 0] >= 0).astype(F32)
    inverse = lax.rsqrt(variance + 1e-05) * row_live
    stats = jnp.stack([inverse, -mean_value * inverse, row_live]).reshape(3, devices_req, capacity)
    stats = lax.all_to_all(stats, "req", split_axis=1, concat_axis=1, tiled=True)
    stats = stats.reshape(3, devices_req * capacity, 1, 1)

    arrived = arrived.reshape(devices_req * capacity, 4, quarter).astype(F32)
    result = (arrived * stats[0] + stats[1]) * proj_gain + stats[2] * proj_bias
    return result.astype(BF16)


def solution(mesh):
    placed = (
        P("req", None),
        P(),
        P("req", "tp"),
        P("tp"),
        P("tp"),
        P("tp", "req"),
        P("req", None),
        P("req"),
        P(None, "tp"),
        P(None, "tp"),
    )
    return jax.shard_map(
        body, mesh=mesh, in_specs=placed, out_specs=P("req", None, "tp"), check_vma=False
    )
```

```python
import math

import jax
import jax.numpy as jnp
from jax import lax
from jax.experimental import pallas as pl
from jax.experimental.pallas import tpu as pltpu
from jax.sharding import PartitionSpec as P

D = 3200
HEADS = 16
HEAD_DIM = 128
BF16 = jnp.bfloat16
F32 = jnp.float32


def merge_layout(grid, token_count, slot_count):
    half_rows = grid[:, 0]
    half_cols = grid[:, 1]
    image_slots = half_rows * half_cols
    slot_ends = jnp.cumsum(image_slots)
    slot_starts = slot_ends - image_slots
    slot_ids = jnp.arange(slot_count, dtype=jnp.int32)
    image_ids = jnp.sum((slot_ids[:, None] >= slot_ends[None, :]).astype(jnp.int32), axis=1)
    image_count = grid.shape[0]
    is_live = image_ids < image_count
    one_hot = (image_ids[:, None] == jnp.arange(image_count, dtype=jnp.int32)[None, :]).astype(
        jnp.int32
    )
    cols_here = jnp.maximum(jnp.sum(one_hot * half_cols[None, :], axis=1), 1)
    start_here = jnp.sum(one_hot * slot_starts[None, :], axis=1)
    offset = slot_ids - start_here
    row_half = offset // cols_here
    col_half = offset % cols_here
    first_row = 4 * start_here + 4 * row_half * cols_here + 2 * col_half
    patch_rows = jnp.stack(
        [first_row, first_row + 1, first_row + 2 * cols_here, first_row + 2 * cols_here + 1], axis=1
    )
    patch_rows = jnp.where(is_live[:, None], patch_rows, 0)
    token_ids = jnp.arange(token_count, dtype=jnp.int32)
    segment = jnp.sum((token_ids[:, None] >= 4 * slot_ends[None, :]).astype(jnp.int32), axis=1)
    return (patch_rows, is_live, segment)


def owner_ranks(owner_ids, is_live):
    slot_ids = jnp.arange(owner_ids.shape[0], dtype=jnp.int32)
    earlier = (
        (owner_ids[:, None] == owner_ids[None, :])
        & (slot_ids[None, :] < slot_ids[:, None])
        & is_live[None, :]
    )
    return jnp.sum(earlier.astype(jnp.int32), axis=1)


def dest_tokens(patch_rows, is_live, owners, ranks, capacity, devices_req, first):
    target = jnp.where(is_live, (owners ^ first) * capacity + ranks, -1)
    rows = jnp.arange(devices_req * capacity, dtype=jnp.int32)
    hit = (target[None, :] == rows[:, None]).astype(jnp.int32)
    return jnp.sum(hit[:, :, None] * (patch_rows[None] + 1), axis=1) - 1


def swap(value, axis, bit):
    count = lax.axis_size(axis)
    return lax.ppermute(value, axis, [(i, i ^ bit) for i in range(count)])


def ring(value):
    count = lax.axis_size("req")
    return lax.ppermute(value, "req", [(i, (i + 2) % count) for i in range(count)])


def call(kernel, name, out, operands, flops, scalars=0, raw=0, scratch=()):
    def whole(x):
        return pl.BlockSpec(x.shape, lambda i: (0,) * len(x.shape))

    blocks = operands[scalars : len(operands) - raw]
    moved = sum(x.size * x.dtype.itemsize for x in operands[scalars:] + tuple(out))
    return pl.pallas_call(
        kernel,
        grid=(1,),
        out_shape=tuple(out),
        in_specs=[pl.BlockSpec(memory_space=pltpu.SMEM)] * scalars
        + [whole(x) for x in blocks]
        + [pl.BlockSpec(memory_space=pl.ANY)] * raw,
        out_specs=tuple(whole(x) for x in out),
        scratch_shapes=scratch,
        compiler_params=pltpu.CompilerParams(vmem_limit_bytes=32 << 20),
        cost_estimate=pl.CostEstimate(flops=flops, bytes_accessed=moved, transcendentals=0),
        name=name,
    )(*operands)


def array(shape, dtype):
    return jax.ShapeDtypeStruct(shape, dtype)


def split_kernel(w_ref, q_ref, k_ref, v_ref):
    for head in range(q_ref.shape[1] // HEAD_DIM):
        to = pl.ds(head * HEAD_DIM, HEAD_DIM)
        for i, ref in enumerate((q_ref, k_ref, v_ref)):
            ref[:, to] = w_ref[:, pl.ds((3 * head + i) * HEAD_DIM, HEAD_DIM)]


def norm_kernel(side_ref, tokens_ref, gain_ref, mine_ref, others_ref):
    rows, width = tokens_ref.shape
    depth = width // 8
    step = 48

    @pl.loop(0, rows // step)
    def _(i):
        at = pl.ds(pl.multiple_of(i * step, step), step)
        values = tokens_ref[at, :].astype(F32)
        inverse = lax.rsqrt(jnp.mean(values * values, axis=1, keepdims=True) + 1e-06)
        normed = values * inverse * gain_ref[...]
        for plane in range(width // (2 * depth)):
            low = normed[:, 2 * plane * depth : (2 * plane + 1) * depth]
            high = normed[:, (2 * plane + 1) * depth : (2 * plane + 2) * depth]
            to = pl.ds(plane * depth, depth)
            mine_ref[at, to] = jnp.where(side_ref[0] == 0, low, high).astype(BF16)
            others_ref[at, to] = jnp.where(side_ref[0] == 0, high, low).astype(BF16)
        filled = mine_ref.shape[1]
        others_ref[at, filled:] = jnp.zeros((step, others_ref.shape[1] - filled), BF16)


def norm_tokens(side, tokens, norm_gain):
    rows, columns = tokens.shape[0], tokens.shape[1] // 2
    out = (array((rows, columns), BF16), array((rows, pl.cdiv(columns, 128) * 128), BF16))
    return call(norm_kernel, "norm_tokens", out, (side, tokens, norm_gain[None]), 0, scalars=1)


def place_blocks(plane, block_refs, weights_ref, sems):
    count, depth = len(block_refs), block_refs[0].shape[0]
    copies = []
    for i, ref in enumerate(block_refs):
        first = lax.rem(plane + count - i, count) * depth
        to = weights_ref.at[pl.ds(pl.multiple_of(first, 16), depth), :]
        copies.append(pltpu.make_async_copy(ref, to, sems.at[i]))
    for copy in copies:
        copy.start()
    for copy in copies:
        copy.wait()


def project_kernel(plane_ref, mine_ref, theirs_ref, *refs):
    *block_refs, own_ref, peer_ref, weights_ref, sems = refs
    place_blocks(plane_ref[0], block_refs, weights_ref, sems)
    weights = weights_ref[...]
    theirs = theirs_ref[:, : weights.shape[0]]
    peer_ref[...] = jnp.dot(theirs, weights, preferred_element_type=F32).astype(BF16)
    own_ref[...] = jnp.dot(mine_ref[...], weights, preferred_element_type=F32)


def project(plane, mine, theirs, blocks):
    rows, columns = mine.shape[0], blocks[0].shape[1]
    depth = blocks[0].shape[0] * len(blocks)
    return call(
        project_kernel,
        "project",
        (array((rows, columns), F32), array((rows, columns), BF16)),
        (plane, mine, theirs, *blocks),
        4 * rows * depth * columns,
        scalars=1,
        raw=len(blocks),
        scratch=(
            pltpu.VMEM((depth, columns), BF16),
            pltpu.SemaphoreType.DMA((len(blocks),)),
        ),
    )


def scores_kernel(q_ref, q_got_ref, k_ref, k_got_ref, q_gain_ref, k_gain_ref, raw_ref, sums_ref):
    queries = q_ref[...] + q_got_ref[...].astype(F32)
    key_vecs = k_ref[...] + k_got_ref[...].astype(F32)
    sums_ref[:, 0:1] = jnp.sum(queries * queries, axis=1, keepdims=True)
    sums_ref[:, 1:2] = jnp.sum(key_vecs * key_vecs, axis=1, keepdims=True)
    queries = queries * (q_gain_ref[...] * (1.0 / math.sqrt(HEAD_DIM)))
    key_vecs = key_vecs * k_gain_ref[...]
    for head in range(raw_ref.shape[0]):
        part = slice(head * HEAD_DIM, (head + 1) * HEAD_DIM)
        raw_ref[head] = lax.dot_general(
            queries[:, part],
            key_vecs[:, part],
            (((1,), (1,)), ((), ())),
            precision=lax.Precision.HIGHEST,
            preferred_element_type=F32,
        )


def attend_kernel(raw_ref, q_scale_ref, k_scale_ref, seg_ref, seg_row_ref, v_ref, v_got_ref, out_ref):
    same = seg_ref[...] == seg_row_ref[...]
    values = (v_ref[...] + v_got_ref[...].astype(F32)).astype(BF16)
    for head in range(raw_ref.shape[0]):
        part = slice(head * HEAD_DIM, (head + 1) * HEAD_DIM)
        scores = raw_ref[head] * q_scale_ref[...] * k_scale_ref[...]
        scores = jnp.where(same, scores, -1e30)
        raised = jnp.exp(scores - jnp.max(scores, axis=1, keepdims=True))
        probs = (raised / jnp.sum(raised, axis=1, keepdims=True)).astype(BF16)
        out_ref[:, part] = jnp.dot(
            probs, values[:, part], preferred_element_type=F32
        ).astype(BF16)


def project_out_kernel(place_ref, attended_ref, *refs):
    *block_refs, sent_ref, kept_far_ref, kept_ref, weights_ref, sems = refs
    depth = block_refs[0].shape[0]
    place_blocks(place_ref[0], block_refs, weights_ref, sems)
    column = place_ref[2]
    attended = attended_ref[...]

    def term(index):
        rows = weights_ref[pl.ds(pl.multiple_of(index * depth, 16), depth), :]
        return lax.dot_general(
            rows, attended, (((1,), (1,)), ((), ())), preferred_element_type=F32
        )

    sent_ref[0] = term(column ^ 3).astype(BF16)
    sent_ref[1] = term(column ^ 1).astype(BF16)
    kept_far_ref[...] = term(column ^ 2)
    kept_ref[...] = term(column)


def project_out(place, attended, blocks):
    rows = attended.shape[0]
    depth, width = blocks[0].shape
    kept = array((depth, rows), F32)
    return call(
        project_out_kernel,
        "project_out",
        (array((2, depth, rows), BF16), kept, kept),
        (place, attended, *blocks),
        2 * rows * depth * width * len(blocks),
        scalars=1,
        raw=len(blocks),
        scratch=(
            pltpu.VMEM((depth * len(blocks), width), BF16),
            pltpu.SemaphoreType.DMA((len(blocks),)),
        ),
    )


def far_kernel(kept_ref, near_ref, far_ref):
    far_ref[...] = (kept_ref[...] + near_ref[0].astype(F32)).astype(BF16)


def pack_kernel(kept_ref, near_ref, far_ref, token_ref, chosen_ref, sums_ref, *block_refs):
    attn_out = kept_ref[...] + near_ref[1].astype(F32) + far_ref[...].astype(F32)
    hidden = (token_ref[...].astype(F32) + attn_out).astype(BF16)
    depth = hidden.shape[0]
    rows = block_refs[0].shape[0]
    for patch in range(4):
        first = patch * rows * len(block_refs)
        picked = lax.dot_general(
            chosen_ref[pl.ds(first, rows * len(block_refs)), :],
            hidden,
            (((1,), (1,)), ((), ())),
            preferred_element_type=F32,
        )
        for i, ref in enumerate(block_refs):
            part = picked[i * rows : (i + 1) * rows]
            ref[:, pl.ds(patch * depth, depth)] = part.astype(BF16)
    hidden = hidden.astype(F32)
    sums_ref[0:1, :] = jnp.sum(hidden, axis=0, keepdims=True)
    sums_ref[1:2, :] = jnp.sum(hidden * hidden, axis=0, keepdims=True)


def pack(kept, near, far, token_part, chosen, count):
    depth, token_count = far.shape
    rows = chosen.shape[0] // 4 // count
    out = (array((2, token_count), F32),) + (array((rows, 4 * depth), BF16),) * count
    operands = (kept, near, far, token_part, chosen)
    return call(pack_kernel, "pack", out, operands, 2 * chosen.size * depth)


def finish_kernel(place_ref, stats_ref, gain_ref, bias_ref, *refs):
    out_ref = refs[-1]
    count = (len(refs) - 1) // 2
    rows, _, quarter = out_ref.shape
    rows = rows // count
    depth = quarter // 2
    for i in range(count):
        source = place_ref[0] ^ i
        to = pl.ds(source * rows, rows)
        swapped = (source & 1) == 1
        scale, shift, live = (stats_ref[j, to][:, 0:1] for j in range(3))
        for patch in range(4):
            part = slice(patch * depth, (patch + 1) * depth)
            own = refs[i][:, part].astype(F32)
            other = refs[count + i][:, part].astype(F32)
            values = jnp.concatenate(
                [jnp.where(swapped, other, own), jnp.where(swapped, own, other)], axis=1
            )
            gain, bias = gain_ref[patch : patch + 1, :], bias_ref[patch : patch + 1, :]
            values = (values * scale + shift) * gain + live * bias
            out_ref[to, patch, :] = values.astype(BF16)


def finish(me, stats, proj_gain, proj_bias, blocks):
    rows = stats.shape[1]
    stats = jnp.broadcast_to(stats[:, :, None], (3, rows, 128))
    out = array((rows,) + proj_gain.shape, BF16)
    operands = (me.reshape(1), stats, proj_gain, proj_bias) + tuple(blocks)
    return call(finish_kernel, "finish", (out,), operands, 6 * out.size, scalars=1)[0]


def after(value, *first):
    return lax.optimization_barrier((value,) + first)[0]


def general_body(tokens, norm_gain, w_qkv, q_gain, k_gain, w_out, grids, owners, proj_gain, proj_bias):
    token_count = tokens.shape[0]
    slot_count = owners.shape[0]
    quarter = proj_gain.shape[1]
    head_share = q_gain.shape[0]
    head_count = head_share // HEAD_DIM
    head_width = HEADS * HEAD_DIM
    score_scale = 1.0 / math.sqrt(HEAD_DIM)
    feature_total = 4 * D
    devices_req = lax.axis_size("req")
    capacity = max(2, (2 * slot_count + devices_req - 1) // devices_req)
    patch_rows, is_live, segment = merge_layout(grids, token_count, slot_count)
    token_float = tokens.astype(jnp.float32)
    mean_square = jnp.mean(token_float * token_float, axis=1, keepdims=True)
    normed = (token_float * lax.rsqrt(mean_square + 1e-06) * norm_gain).astype(jnp.bfloat16)
    projected = jnp.dot(
        normed, lax.all_gather(w_qkv, "req", axis=0, tiled=True), preferred_element_type=jnp.float32
    )
    projected = projected.reshape(token_count, head_count, 3, HEAD_DIM)
    queries = projected[:, :, 0]
    key_vecs = projected[:, :, 1]
    values = projected[:, :, 2].astype(jnp.bfloat16)
    q_gains = q_gain.reshape(head_count, HEAD_DIM)
    k_gains = k_gain.reshape(head_count, HEAD_DIM)
    local_q = jnp.sum(queries * queries, axis=(1, 2))
    local_k = jnp.sum(key_vecs * key_vecs, axis=(1, 2))
    q_total, k_total = lax.psum((local_q, local_k), "tp")
    q_scale = lax.rsqrt(q_total / head_width + 1e-06)
    k_scale = lax.rsqrt(k_total / head_width + 1e-06)
    q_normed = queries * q_scale[:, None, None] * q_gains
    k_normed = key_vecs * k_scale[:, None, None] * k_gains
    scores = (
        jnp.einsum("qhd,khd->hqk", q_normed, k_normed, precision=lax.Precision.HIGHEST)
        * score_scale
    )
    same_image = segment[:, None] == segment[None, :]
    scores = jnp.where(same_image[None], scores, -1e30)
    row_top = jnp.max(scores, axis=2, keepdims=True)
    weights_raw = jnp.exp(scores - row_top)
    probs = (weights_raw / jnp.sum(weights_raw, axis=2, keepdims=True)).astype(jnp.bfloat16)
    attended = jnp.einsum("hqk,khd->qhd", probs, values, preferred_element_type=jnp.float32)
    attended = attended.astype(jnp.bfloat16).reshape(token_count, head_share)
    partial_sum = jnp.dot(
        attended,
        lax.all_gather(w_out, "req", axis=1, tiled=True),
        preferred_element_type=jnp.float32,
    )
    mine = lax.psum_scatter(
        partial_sum.astype(jnp.bfloat16), "tp", scatter_dimension=1, tiled=True
    ).astype(jnp.float32)
    token_mine = lax.dynamic_slice_in_dim(token_float, lax.axis_index("tp") * quarter, quarter, 1)
    hidden = (token_mine + mine).astype(jnp.bfloat16)
    merged = jnp.where(is_live[:, None, None], hidden[patch_rows], jnp.zeros((), jnp.bfloat16))
    ranks = owner_ranks(owners, is_live)
    target_owner = jnp.where(is_live, owners, devices_req)
    send_slots = jnp.zeros((devices_req, capacity, 4, quarter), jnp.bfloat16)
    send_slots = send_slots.at[target_owner, ranks].set(merged, mode="drop")
    owner_ids = jnp.arange(devices_req, dtype=jnp.int32)
    dest_counts = jnp.sum(
        ((owners[None, :] == owner_ids[:, None]) & is_live[None, :]).astype(jnp.int32), axis=1
    )
    dest_counts = dest_counts[:, None]
    arrived, source_counts = (
        lax.all_to_all(send_slots, "req", split_axis=0, concat_axis=0, tiled=True),
        lax.all_to_all(dest_counts, "req", split_axis=0, concat_axis=0, tiled=True),
    )
    slot_live = jnp.arange(capacity, dtype=jnp.int32)[None, :] < source_counts
    arrived_float = arrived.astype(jnp.float32)
    row_sum = jnp.sum(arrived_float, axis=(2, 3))
    row_sq = jnp.sum(arrived_float * arrived_float, axis=(2, 3))
    row_sum, row_sq = lax.psum((row_sum, row_sq), "tp")
    mean_value = row_sum / feature_total
    variance = row_sq / feature_total - mean_value * mean_value
    normed_out = (arrived_float - mean_value[:, :, None, None]) * lax.rsqrt(variance + 1e-05)[
        :, :, None, None
    ] * proj_gain + proj_bias
    normed_out = jnp.where(slot_live[:, :, None, None], normed_out, 0.0).astype(jnp.bfloat16)
    result = normed_out.reshape(devices_req * capacity, 4, quarter)
    return result


def body(tokens, norm_gain, w_qkv, q_gain, k_gain, w_out, grids, owners, proj_gain, proj_bias):
    token_count = tokens.shape[0]
    slot_count = owners.shape[0]
    quarter = proj_gain.shape[1]
    head_share = q_gain.shape[0]
    head_count = head_share // HEAD_DIM
    head_width = HEADS * HEAD_DIM
    feature_total = 4 * D
    devices_req = lax.axis_size("req")
    devices_tp = lax.axis_size("tp")
    planes = devices_req // 2
    capacity = max(2, (2 * slot_count + devices_req - 1) // devices_req)
    me = lax.axis_index("req")
    plane, side = me // 2, me % 2
    column = lax.axis_index("tp")
    token_ids = jnp.arange(token_count, dtype=jnp.int32)

    part = array((w_qkv.shape[0], head_share), BF16)
    w_q, w_k, w_v = call(split_kernel, "split_heads", (part,) * 3, (w_qkv,), 0)
    w_o = w_out.T
    q_blocks, k_blocks = [w_q], [w_k]
    for step in range(1, planes):
        q_blocks.append(ring(q_blocks[-1]))
        k_blocks.append(ring(k_blocks[-1]))
    v_blocks, o_blocks = [after(w_v, k_blocks[-2])], [after(w_o, q_blocks[-1])]
    for step in range(1, planes):
        v_blocks.append(ring(v_blocks[-1]))
        o_blocks.append(ring(o_blocks[-1]))

    patch_rows, is_live, segment = merge_layout(grids, token_count, slot_count)
    ranks = owner_ranks(owners, is_live)
    placing = (patch_rows, is_live, owners, ranks, capacity, devices_req)
    sent_tokens = dest_tokens(*placing, me)
    chosen = (sent_tokens.T.reshape(-1)[:, None] == token_ids[None, :]).astype(BF16)
    row_tokens = dest_tokens(*placing, 0)
    in_row = jnp.any(row_tokens[:, :, None] == token_ids[None, None, :], axis=1).astype(F32)
    row_live = (row_tokens[:, 0] >= 0).astype(F32)
    token_mine = lax.dynamic_slice_in_dim(tokens, column * quarter, quarter, 1).T
    token_mine = token_mine.reshape(2, quarter // 2, token_count)

    places = jnp.stack([plane, side, column]).astype(jnp.int32)
    mine, others = norm_tokens(places[1:2], tokens, norm_gain)
    theirs = swap(others, "req", 1)

    def projected(blocks):
        own, peer = project(places[0:1], mine, theirs, blocks)
        return own, swap(peer, "req", 1)

    queries = projected(q_blocks)
    key_vecs = projected(k_blocks)
    values = projected(v_blocks)
    raw, sums = call(
        scores_kernel,
        "scores",
        (
            array((head_count, token_count, token_count), F32),
            array((token_count, 2), F32),
        ),
        (after(queries[0], values[0]), queries[1], *key_vecs, q_gain[None], k_gain[None]),
        12 * token_count * token_count * head_share,
    )
    sums = after(sums, o_blocks[-2])
    scales = lax.rsqrt(lax.psum(sums.T, "tp") / head_width + 1e-06)
    (attended,) = call(
        attend_kernel,
        "attend",
        (array((token_count, head_share), BF16),),
        (
            after(raw, o_blocks[-1]),
            scales[0][:, None],
            scales[1][None],
            segment[:, None],
            segment[None],
            *values,
        ),
        2 * token_count * token_count * head_share,
    )

    halves, token_sums = [], 0.0
    others_blocks = [swap(block, "req", 1) for block in o_blocks]
    for half, blocks in ((side, o_blocks), (1 - side, others_blocks)):
        sent, kept_far, kept = project_out(places, attended, blocks)
        near = swap(sent, "tp", 1)
        (far,) = call(far_kernel, "far_sum", (array(kept.shape, BF16),), (kept_far, near), 0)
        far = swap(far, "tp", 2)
        token_part = lax.dynamic_index_in_dim(token_mine, half, 0, keepdims=False)
        sums, *blocks = pack(kept, near, far, token_part, chosen, devices_req)
        for bits in reversed(range(1, devices_req)):
            blocks[bits] = swap(blocks[bits], "req", bits)
        halves += blocks
        token_sums = token_sums + sums

    token_sums = token_sums + sum(swap(token_sums, "tp", bit) for bit in range(1, devices_tp))
    row_sums = jnp.sum(in_row[None] * token_sums[:, None, :], axis=2)
    mean_value = row_sums[0] / feature_total
    variance = row_sums[1] / feature_total - mean_value * mean_value
    inverse = lax.rsqrt(variance + 1e-05) * row_live
    stats = jnp.stack([inverse, -mean_value * inverse, row_live]).reshape(3, devices_req, capacity)
    stats = lax.all_to_all(stats, "req", split_axis=1, concat_axis=1, tiled=True)
    stats = stats.reshape(3, devices_req * capacity)
    return finish(me, stats, proj_gain, proj_bias, halves)


def solution(mesh):
    placed = (
        P("req", None),
        P(),
        P("req", "tp"),
        P("tp"),
        P("tp"),
        P("tp", "req"),
        P("req", None),
        P("req"),
        P(None, "tp"),
        P(None, "tp"),
    )
    planes, odd = divmod(mesh.shape["req"], 2)
    fits = not odd and planes == mesh.shape["tp"] == 4
    return jax.shard_map(
        body if fits else general_body, mesh=mesh, in_specs=placed, out_specs=P("req", None, "tp"), check_vma=False
    )
```

```python
import math

import jax
import jax.numpy as jnp
from jax import lax
from jax.experimental import pallas as pl
from jax.experimental.pallas import tpu as pltpu
from jax.sharding import PartitionSpec as P

D = 3200
HEADS = 16
HEAD_DIM = 128
BF16 = jnp.bfloat16
F32 = jnp.float32


def merge_layout(grid, token_count, slot_count):
    half_rows = grid[:, 0]
    half_cols = grid[:, 1]
    image_slots = half_rows * half_cols
    slot_ends = jnp.cumsum(image_slots)
    slot_starts = slot_ends - image_slots
    slot_ids = jnp.arange(slot_count, dtype=jnp.int32)
    image_ids = jnp.sum((slot_ids[:, None] >= slot_ends[None, :]).astype(jnp.int32), axis=1)
    image_count = grid.shape[0]
    is_live = image_ids < image_count
    one_hot = (image_ids[:, None] == jnp.arange(image_count, dtype=jnp.int32)[None, :]).astype(
        jnp.int32
    )
    cols_here = jnp.maximum(jnp.sum(one_hot * half_cols[None, :], axis=1), 1)
    start_here = jnp.sum(one_hot * slot_starts[None, :], axis=1)
    offset = slot_ids - start_here
    row_half = offset // cols_here
    col_half = offset % cols_here
    first_row = 4 * start_here + 4 * row_half * cols_here + 2 * col_half
    patch_rows = jnp.stack(
        [first_row, first_row + 1, first_row + 2 * cols_here, first_row + 2 * cols_here + 1], axis=1
    )
    patch_rows = jnp.where(is_live[:, None], patch_rows, 0)
    token_ids = jnp.arange(token_count, dtype=jnp.int32)
    segment = jnp.sum((token_ids[:, None] >= 4 * slot_ends[None, :]).astype(jnp.int32), axis=1)
    return (patch_rows, is_live, segment)


def owner_ranks(owner_ids, is_live):
    slot_ids = jnp.arange(owner_ids.shape[0], dtype=jnp.int32)
    earlier = (
        (owner_ids[:, None] == owner_ids[None, :])
        & (slot_ids[None, :] < slot_ids[:, None])
        & is_live[None, :]
    )
    return jnp.sum(earlier.astype(jnp.int32), axis=1)


def dest_tokens(patch_rows, is_live, owners, ranks, capacity, devices_req):
    target = jnp.where(is_live, owners * capacity + ranks, -1)
    rows = jnp.arange(devices_req * capacity, dtype=jnp.int32)
    hit = (target[None, :] == rows[:, None]).astype(jnp.int32)
    return jnp.sum(hit[:, :, None] * (patch_rows[None] + 1), axis=1) - 1


def swap(value, axis, bit):
    count = lax.axis_size(axis)
    return lax.ppermute(value, axis, [(i, i ^ bit) for i in range(count)])


def ring(value, step=1):
    count = lax.axis_size("req")
    return lax.ppermute(value, "req", [(i, (i + 2 * step) % count) for i in range(count)])


def call(kernel, name, out, operands, flops, scalars=0, raw=0, scratch=(), ties=()):
    used = len(operands)
    operands = tuple(operands) + tuple(x[:8, :128] for x in ties)
    raw = raw + len(ties)

    def untied(*refs):
        kernel(*refs[:used], *refs[used + len(ties) :])

    def whole(x):
        return pl.BlockSpec(x.shape, lambda i: (0,) * len(x.shape))

    blocks = operands[scalars : len(operands) - raw]
    moved = sum(x.size * x.dtype.itemsize for x in operands[scalars:] + tuple(out))
    return pl.pallas_call(
        untied,
        grid=(1,),
        out_shape=tuple(out),
        in_specs=[pl.BlockSpec(memory_space=pltpu.SMEM)] * scalars
        + [whole(x) for x in blocks]
        + [pl.BlockSpec(memory_space=pl.ANY)] * raw,
        out_specs=tuple(whole(x) for x in out),
        scratch_shapes=scratch,
        compiler_params=pltpu.CompilerParams(vmem_limit_bytes=20 << 20),
        cost_estimate=pl.CostEstimate(flops=flops, bytes_accessed=moved, transcendentals=0),
        name=name,
    )(*operands)


def array(shape, dtype):
    return jax.ShapeDtypeStruct(shape, dtype)


def split_kernel(w_ref, q_ref, k_ref, v_ref):
    for head in range(q_ref.shape[1] // HEAD_DIM):
        to = pl.ds(head * HEAD_DIM, HEAD_DIM)
        for i, ref in enumerate((q_ref, k_ref, v_ref)):
            ref[:, to] = w_ref[:, pl.ds((3 * head + i) * HEAD_DIM, HEAD_DIM)]


def norm_kernel(side_ref, tokens_ref, gain_ref, mine_ref, others_ref):
    rows, width = tokens_ref.shape
    depth = width // 8
    step = 48

    @pl.loop(0, rows // step)
    def _(i):
        at = pl.ds(pl.multiple_of(i * step, step), step)
        values = tokens_ref[at, :].astype(F32)
        inverse = lax.rsqrt(jnp.mean(values * values, axis=1, keepdims=True) + 1e-06)
        normed = values * inverse * gain_ref[...]
        for plane in range(width // (2 * depth)):
            low = normed[:, 2 * plane * depth : (2 * plane + 1) * depth]
            high = normed[:, (2 * plane + 1) * depth : (2 * plane + 2) * depth]
            to = pl.ds(plane * depth, depth)
            mine_ref[at, to] = jnp.where(side_ref[0] == 0, low, high).astype(BF16)
            others_ref[at, to] = jnp.where(side_ref[0] == 0, high, low).astype(BF16)
        filled = mine_ref.shape[1]
        others_ref[at, filled:] = jnp.zeros((step, others_ref.shape[1] - filled), BF16)


def norm_tokens(side, tokens, norm_gain):
    rows, columns = tokens.shape[0], tokens.shape[1] // 2
    out = (array((rows, columns), BF16), array((rows, pl.cdiv(columns, 128) * 128), BF16))
    return call(norm_kernel, "norm_tokens", out, (side, tokens, norm_gain[None]), 0, scalars=1)


def place_blocks(plane, block_refs, weights_ref, sems):
    count, depth = len(block_refs), block_refs[0].shape[0]
    copies = []
    for i, ref in enumerate(block_refs):
        first = lax.rem(plane + count - i, count) * depth
        to = weights_ref.at[pl.ds(pl.multiple_of(first, 16), depth), :]
        copies.append(pltpu.make_async_copy(ref, to, sems.at[i]))
    for copy in copies:
        copy.start()
    for copy in copies:
        copy.wait()


def project_kernel(plane_ref, mine_ref, theirs_ref, *refs):
    *block_refs, own_ref, peer_ref, weights_ref, sems = refs
    place_blocks(plane_ref[0], block_refs, weights_ref, sems)
    weights = weights_ref[...]
    theirs = theirs_ref[:, : weights.shape[0]]
    peer_ref[...] = jnp.dot(theirs, weights, preferred_element_type=F32).astype(BF16)
    own_ref[...] = jnp.dot(mine_ref[...], weights, preferred_element_type=F32)


def project(plane, mine, theirs, blocks):
    rows, columns = mine.shape[0], blocks[0].shape[1]
    depth = blocks[0].shape[0] * len(blocks)
    return call(
        project_kernel,
        "project",
        (array((rows, columns), F32), array((rows, columns), BF16)),
        (plane, mine, theirs, *blocks),
        4 * rows * depth * columns,
        scalars=1,
        raw=len(blocks),
        scratch=(
            pltpu.VMEM((depth, columns), BF16),
            pltpu.SemaphoreType.DMA((len(blocks),)),
        ),
    )


def scores_kernel(q_ref, q_got_ref, k_ref, k_got_ref, q_gain_ref, k_gain_ref, raw_ref, sums_ref):
    share = q_ref.shape[1]
    queries = q_ref[...] + q_got_ref[...].astype(F32)
    key_vecs = k_ref[...] + k_got_ref[...].astype(F32)
    ones = jnp.ones((8, share), F32)
    for i, values in enumerate((queries, key_vecs)):
        totals = lax.dot_general(
            ones,
            values * values,
            (((1,), (1,)), ((), ())),
            precision=lax.Precision.HIGHEST,
            preferred_element_type=F32,
        )
        sums_ref[i : i + 1, :] = totals[0:1]
    queries = queries * (q_gain_ref[...] * (1.0 / math.sqrt(HEAD_DIM)))
    key_vecs = key_vecs * k_gain_ref[...]
    for head in range(raw_ref.shape[0]):
        part = slice(head * HEAD_DIM, (head + 1) * HEAD_DIM)
        raw_ref[head] = lax.dot_general(
            queries[:, part],
            key_vecs[:, part],
            (((1,), (1,)), ((), ())),
            precision=lax.Precision.HIGHEST,
            preferred_element_type=F32,
        )


def attend_kernel(raw_ref, sums_ref, segment_ref, v_ref, v_got_ref, out_ref):
    rows = raw_ref.shape[1]
    scales = lax.rsqrt(sums_ref[...] / (HEADS * HEAD_DIM) + 1e-06)
    q_scale = jnp.broadcast_to(scales[0:1], (128, rows)).T[:, 0:1]
    k_scale = scales[1:2]
    segment = segment_ref[...]
    same = jnp.broadcast_to(segment, (128, rows)).T[:, 0:1] == segment
    values = (v_ref[...] + v_got_ref[...].astype(F32)).astype(BF16)
    for head in range(raw_ref.shape[0]):
        part = slice(head * HEAD_DIM, (head + 1) * HEAD_DIM)
        scores = raw_ref[head] * q_scale * k_scale
        scores = jnp.where(same, scores, -1e30)
        raised = jnp.exp(scores - jnp.max(scores, axis=1, keepdims=True))
        probs = (raised / jnp.sum(raised, axis=1, keepdims=True)).astype(BF16)
        out_ref[:, part] = jnp.dot(
            probs, values[:, part], preferred_element_type=F32
        ).astype(BF16)


def project_out_kernel(place_ref, attended_ref, *refs):
    *block_refs, sent_ref, kept_far_ref, kept_ref, weights_ref, sems = refs
    depth = block_refs[0].shape[0]
    place_blocks(place_ref[0], block_refs, weights_ref, sems)
    column = place_ref[2]
    attended = attended_ref[...]

    def term(index):
        rows = weights_ref[pl.ds(pl.multiple_of(index * depth, 16), depth), :]
        return lax.dot_general(
            rows, attended, (((1,), (1,)), ((), ())), preferred_element_type=F32
        )

    sent_ref[0] = term(column ^ 3).astype(BF16)
    sent_ref[1] = term(column ^ 1).astype(BF16)
    kept_far_ref[...] = term(column ^ 2)
    kept_ref[...] = term(column)


def project_out(place, attended, blocks):
    rows = attended.shape[0]
    depth, width = blocks[0].shape
    kept = array((depth, rows), F32)
    return call(
        project_out_kernel,
        "project_out",
        (array((2, depth, rows), BF16), kept, kept),
        (place, attended, *blocks),
        2 * rows * depth * width * len(blocks),
        scalars=1,
        raw=len(blocks),
        scratch=(
            pltpu.VMEM((depth * len(blocks), width), BF16),
            pltpu.SemaphoreType.DMA((len(blocks),)),
        ),
    )


def far_kernel(kept_ref, near_ref, far_ref):
    far_ref[...] = (kept_ref[...] + near_ref[0].astype(F32)).astype(BF16)


def hidden_of(kept_ref, near_ref, far_ref, token_ref):
    attn_out = kept_ref[...] + near_ref[1].astype(F32) + far_ref[...].astype(F32)
    return (token_ref[...].astype(F32) + attn_out).astype(BF16)


def sum_tokens(hidden, sums_ref, first=0):
    hidden = hidden.astype(F32)
    sums_ref[first : first + 1, :] = jnp.sum(hidden, axis=0, keepdims=True)
    sums_ref[first + 1 : first + 2, :] = jnp.sum(hidden * hidden, axis=0, keepdims=True)


def hidden_kernel(kept_ref, near_ref, far_ref, token_ref, hidden_ref, sums_ref):
    hidden = hidden_of(kept_ref, near_ref, far_ref, token_ref)
    hidden_ref[...] = hidden
    sum_tokens(hidden, sums_ref)


def pack_kernel(
    first_ref, first_sums_ref, kept_ref, near_ref, far_ref, token_ref, own_ref, next_ref,
    rows_ref, sums_ref,
):
    halves = [first_ref[...], hidden_of(kept_ref, near_ref, far_ref, token_ref)]
    depth = halves[0].shape[0]
    count, rows, _ = rows_ref.shape
    rows = rows // 2
    for patch in range(4):
        for half, (hidden, chosen_ref) in enumerate(zip(halves, (own_ref, next_ref))):
            chosen = chosen_ref[pl.ds(patch * rows * count, rows * count), :]
            picked = lax.dot_general(
                chosen, hidden, (((1,), (1,)), ((), ())), preferred_element_type=F32
            )
            picked = picked.reshape(count, rows, depth).astype(BF16)
            rows_ref[:, pl.ds(half * rows, rows), pl.ds(patch * depth, depth)] = picked
    sums_ref[0:2, :] = first_sums_ref[...]
    sum_tokens(halves[1], sums_ref, 2)


def finish_kernel(stats_ref, gain_ref, bias_ref, rows_ref, out_ref):
    count, rows, _ = rows_ref.shape
    rows = rows // 2
    depth = out_ref.shape[2] // 2
    for i in range(count):
        to = pl.ds(i * rows, rows)
        scale, shift, live = (stats_ref[j, to][:, 0:1] for j in range(3))
        for patch in range(4):
            part = slice(patch * depth, (patch + 1) * depth)
            parts = [rows_ref[i, :rows, part].astype(F32), rows_ref[i ^ 1, rows:, part].astype(F32)]
            values = jnp.concatenate(parts[::-1] if i % 2 else parts, axis=1)
            gain, bias = gain_ref[patch : patch + 1, :], bias_ref[patch : patch + 1, :]
            values = (values * scale + shift) * gain + live * bias
            out_ref[to, patch, :] = values.astype(BF16)


def finish(stats, proj_gain, proj_bias, arrived):
    rows = stats.shape[1]
    stats = jnp.broadcast_to(stats[:, :, None], (3, rows, 128))
    out = array((rows,) + proj_gain.shape, BF16)
    operands = (stats, proj_gain, proj_bias, arrived)
    return call(finish_kernel, "finish", (out,), operands, 6 * out.size)[0]


def after(value, *first):
    return lax.optimization_barrier((value,) + first)[0]


def general_body(tokens, norm_gain, w_qkv, q_gain, k_gain, w_out, grids, owners, proj_gain, proj_bias):
    token_count = tokens.shape[0]
    slot_count = owners.shape[0]
    quarter = proj_gain.shape[1]
    head_share = q_gain.shape[0]
    head_count = head_share // HEAD_DIM
    head_width = HEADS * HEAD_DIM
    score_scale = 1.0 / math.sqrt(HEAD_DIM)
    feature_total = 4 * D
    devices_req = lax.axis_size("req")
    capacity = max(2, (2 * slot_count + devices_req - 1) // devices_req)
    patch_rows, is_live, segment = merge_layout(grids, token_count, slot_count)
    token_float = tokens.astype(jnp.float32)
    mean_square = jnp.mean(token_float * token_float, axis=1, keepdims=True)
    normed = (token_float * lax.rsqrt(mean_square + 1e-06) * norm_gain).astype(jnp.bfloat16)
    projected = jnp.dot(
        normed, lax.all_gather(w_qkv, "req", axis=0, tiled=True), preferred_element_type=jnp.float32
    )
    projected = projected.reshape(token_count, head_count, 3, HEAD_DIM)
    queries = projected[:, :, 0]
    key_vecs = projected[:, :, 1]
    values = projected[:, :, 2].astype(jnp.bfloat16)
    q_gains = q_gain.reshape(head_count, HEAD_DIM)
    k_gains = k_gain.reshape(head_count, HEAD_DIM)
    local_q = jnp.sum(queries * queries, axis=(1, 2))
    local_k = jnp.sum(key_vecs * key_vecs, axis=(1, 2))
    q_total, k_total = lax.psum((local_q, local_k), "tp")
    q_scale = lax.rsqrt(q_total / head_width + 1e-06)
    k_scale = lax.rsqrt(k_total / head_width + 1e-06)
    q_normed = queries * q_scale[:, None, None] * q_gains
    k_normed = key_vecs * k_scale[:, None, None] * k_gains
    scores = (
        jnp.einsum("qhd,khd->hqk", q_normed, k_normed, precision=lax.Precision.HIGHEST)
        * score_scale
    )
    same_image = segment[:, None] == segment[None, :]
    scores = jnp.where(same_image[None], scores, -1e30)
    row_top = jnp.max(scores, axis=2, keepdims=True)
    weights_raw = jnp.exp(scores - row_top)
    probs = (weights_raw / jnp.sum(weights_raw, axis=2, keepdims=True)).astype(jnp.bfloat16)
    attended = jnp.einsum("hqk,khd->qhd", probs, values, preferred_element_type=jnp.float32)
    attended = attended.astype(jnp.bfloat16).reshape(token_count, head_share)
    partial_sum = jnp.dot(
        attended,
        lax.all_gather(w_out, "req", axis=1, tiled=True),
        preferred_element_type=jnp.float32,
    )
    mine = lax.psum_scatter(
        partial_sum.astype(jnp.bfloat16), "tp", scatter_dimension=1, tiled=True
    ).astype(jnp.float32)
    token_mine = lax.dynamic_slice_in_dim(token_float, lax.axis_index("tp") * quarter, quarter, 1)
    hidden = (token_mine + mine).astype(jnp.bfloat16)
    merged = jnp.where(is_live[:, None, None], hidden[patch_rows], jnp.zeros((), jnp.bfloat16))
    ranks = owner_ranks(owners, is_live)
    target_owner = jnp.where(is_live, owners, devices_req)
    send_slots = jnp.zeros((devices_req, capacity, 4, quarter), jnp.bfloat16)
    send_slots = send_slots.at[target_owner, ranks].set(merged, mode="drop")
    owner_ids = jnp.arange(devices_req, dtype=jnp.int32)
    dest_counts = jnp.sum(
        ((owners[None, :] == owner_ids[:, None]) & is_live[None, :]).astype(jnp.int32), axis=1
    )
    dest_counts = dest_counts[:, None]
    arrived, source_counts = (
        lax.all_to_all(send_slots, "req", split_axis=0, concat_axis=0, tiled=True),
        lax.all_to_all(dest_counts, "req", split_axis=0, concat_axis=0, tiled=True),
    )
    slot_live = jnp.arange(capacity, dtype=jnp.int32)[None, :] < source_counts
    arrived_float = arrived.astype(jnp.float32)
    row_sum = jnp.sum(arrived_float, axis=(2, 3))
    row_sq = jnp.sum(arrived_float * arrived_float, axis=(2, 3))
    row_sum, row_sq = lax.psum((row_sum, row_sq), "tp")
    mean_value = row_sum / feature_total
    variance = row_sq / feature_total - mean_value * mean_value
    normed_out = (arrived_float - mean_value[:, :, None, None]) * lax.rsqrt(variance + 1e-05)[
        :, :, None, None
    ] * proj_gain + proj_bias
    normed_out = jnp.where(slot_live[:, :, None, None], normed_out, 0.0).astype(jnp.bfloat16)
    result = normed_out.reshape(devices_req * capacity, 4, quarter)
    return result


def body(tokens, norm_gain, w_qkv, q_gain, k_gain, w_out, grids, owners, proj_gain, proj_bias):
    token_count = tokens.shape[0]
    slot_count = owners.shape[0]
    quarter = proj_gain.shape[1]
    head_share = q_gain.shape[0]
    head_count = head_share // HEAD_DIM
    feature_total = 4 * D
    devices_req = lax.axis_size("req")
    planes = devices_req // 2
    capacity = max(2, (2 * slot_count + devices_req - 1) // devices_req)
    me = lax.axis_index("req")
    plane, side = me // 2, me % 2
    column = lax.axis_index("tp")
    token_ids = jnp.arange(token_count, dtype=jnp.int32)

    part = array((w_qkv.shape[0], head_share), BF16)
    w_q, w_k, w_v = call(split_kernel, "split_heads", (part,) * 3, (w_qkv,), 0)
    w_o = w_out.T
    q_up, q_down, k_up = ring(w_q), ring(w_q, -1), ring(w_k)
    k_down = ring(after(w_k, q_up), -1)
    q_far = ring(after(q_up, q_down))
    k_far = ring(k_up)
    v_up = ring(after(w_v, k_down))
    v_down = ring(after(w_v, q_far), -1)
    v_far = ring(v_up)
    o_up = ring(after(w_o, v_up))
    o_down = ring(after(w_o, v_down), -1)
    o_far = ring(o_up)
    q_blocks, k_blocks = [w_q, q_up, q_far, q_down], [w_k, k_up, k_far, k_down]
    v_blocks, o_blocks = [w_v, v_up, v_far, v_down], [w_o, o_up, o_far, o_down]

    own_routes = after(jnp.concatenate([owners, grids.reshape(-1)]), k_down)
    chosen, in_row = [], []
    for routes in (own_routes, swap(own_routes, "req", 1)):
        owner_ids, grid = routes[:slot_count], routes[slot_count:].reshape(-1, 2)
        patch_rows, is_live, tokens_of = merge_layout(grid, token_count, slot_count)
        ranks = owner_ranks(owner_ids, is_live)
        row_tokens = dest_tokens(
            patch_rows, is_live, owner_ids, ranks, capacity, devices_req
        )
        picks = row_tokens.T.reshape(-1)[:, None] == token_ids[None, :]
        chosen.append(picks.astype(BF16))
        picks = row_tokens[:, :, None] == token_ids[None, None, :]
        in_row.append(jnp.any(picks, axis=1).astype(F32))
        if routes is own_routes:
            segment, row_live = tokens_of, (row_tokens[:, 0] >= 0).astype(F32)
    token_mine = lax.dynamic_slice_in_dim(tokens, column * quarter, quarter, 1).T
    token_mine = token_mine.reshape(2, quarter // 2, token_count)
    token_parts = [
        lax.dynamic_index_in_dim(token_mine, side, 0, keepdims=False),
        swap(lax.dynamic_index_in_dim(token_mine, 1 - side, 0, keepdims=False), "req", 1),
    ]

    places = jnp.stack([plane, side, column]).astype(jnp.int32)
    mine, others = norm_tokens(places[1:2], after(tokens, w_q), norm_gain)
    theirs = swap(others, "req", 1)

    mine = after(mine, *token_parts, *chosen)
    queries, q_peer = project(places[0:1], mine, theirs, q_blocks)
    q_got = swap(q_peer, "req", 1)
    key_vecs, k_peer = project(places[0:1], mine, theirs, k_blocks)
    k_got = swap(k_peer, "req", 1)
    values, v_peer = project(places[0:1], mine, theirs, v_blocks)
    v_got = swap(v_peer, "req", 1)
    raw, sums = call(
        scores_kernel,
        "scores",
        (
            array((head_count, token_count, token_count), F32),
            array((2, token_count), F32),
        ),
        (queries, q_got, key_vecs, k_got, q_gain[None], k_gain[None]),
        12 * token_count * token_count * head_share,
        ties=(v_peer,),
    )
    (attended,) = call(
        attend_kernel,
        "attend",
        (array((token_count, head_share), BF16),),
        (raw, lax.psum(sums, "tp"), segment.astype(F32)[None], values, v_got),
        2 * token_count * token_count * head_share,
    )

    parts = []
    for heads_out, token_part in zip((attended, swap(attended, "req", 1)), token_parts):
        sent, kept_far, kept = project_out(places, heads_out, o_blocks)
        near = swap(sent, "tp", 1)
        (far,) = call(far_kernel, "far_sum", (array(kept.shape, BF16),), (kept_far, near), 0)
        parts.append((kept, near, swap(far, "tp", 2), token_part))
    out = (array(kept.shape, BF16), array((2, token_count), F32))
    hidden, own_sums = call(hidden_kernel, "hidden", out, parts[0], 0)
    rows, token_sums = call(
        pack_kernel,
        "pack",
        (array((devices_req, 2 * capacity, 2 * quarter), BF16), array((4, token_count), F32)),
        (hidden, own_sums, *parts[1], *chosen),
        2 * chosen[0].size * quarter,
    )
    arrived = lax.all_to_all(rows, "req", split_axis=0, concat_axis=0, tiled=True)

    token_sums = lax.psum(token_sums, "tp").reshape(2, 2, token_count)
    own_sums, next_sums = (
        jnp.sum(picks[None] * sums[:, None, :], axis=2) for picks, sums in zip(in_row, token_sums)
    )
    got = swap(next_sums, "req", 1)
    row_sums = (own_sums + got) / feature_total
    mean_value = row_sums[0]
    inverse = lax.rsqrt(row_sums[1] - mean_value * mean_value + 1e-05) * row_live
    stats = jnp.stack([inverse, -mean_value * inverse, row_live])
    stats = stats.reshape(3, 1, devices_req, capacity)
    bit = 1
    while bit < devices_req:
        got = swap(stats, "req", bit)
        lower = (me & bit) == 0
        stats = jnp.concatenate(
            [jnp.where(lower, stats, got), jnp.where(lower, got, stats)], axis=1
        )
        bit *= 2
    stats = lax.dynamic_index_in_dim(stats, me, 2, keepdims=False)
    stats = stats.reshape(3, devices_req * capacity)
    return finish(stats, proj_gain, proj_bias, arrived)


def solution(mesh):
    placed = (
        P("req", None),
        P(),
        P("req", "tp"),
        P("tp"),
        P("tp"),
        P("tp", "req"),
        P("req", None),
        P("req"),
        P(None, "tp"),
        P(None, "tp"),
    )
    planes, odd = divmod(mesh.shape["req"], 2)
    fits = not odd and planes == mesh.shape["tp"] == 4
    return jax.shard_map(
        body if fits else general_body, mesh=mesh, in_specs=placed, out_specs=P("req", None, "tp"), check_vma=False
    )
```

```python
import math

import jax
import jax.numpy as jnp
from jax import lax
from jax.experimental import pallas as pl
from jax.experimental.pallas import tpu as pltpu
from jax.sharding import PartitionSpec as P

D = 3200
HEADS = 16
HEAD_DIM = 128
BF16 = jnp.bfloat16
F32 = jnp.float32


def merge_layout(grid, token_count, slot_count):
    half_rows = grid[:, 0]
    half_cols = grid[:, 1]
    image_slots = half_rows * half_cols
    slot_ends = jnp.cumsum(image_slots)
    slot_starts = slot_ends - image_slots
    slot_ids = jnp.arange(slot_count, dtype=jnp.int32)
    image_ids = jnp.sum((slot_ids[:, None] >= slot_ends[None, :]).astype(jnp.int32), axis=1)
    image_count = grid.shape[0]
    is_live = image_ids < image_count
    one_hot = (image_ids[:, None] == jnp.arange(image_count, dtype=jnp.int32)[None, :]).astype(
        jnp.int32
    )
    cols_here = jnp.maximum(jnp.sum(one_hot * half_cols[None, :], axis=1), 1)
    start_here = jnp.sum(one_hot * slot_starts[None, :], axis=1)
    offset = slot_ids - start_here
    row_half = offset // cols_here
    col_half = offset % cols_here
    first_row = 4 * start_here + 4 * row_half * cols_here + 2 * col_half
    patch_rows = jnp.stack(
        [first_row, first_row + 1, first_row + 2 * cols_here, first_row + 2 * cols_here + 1], axis=1
    )
    patch_rows = jnp.where(is_live[:, None], patch_rows, 0)
    token_ids = jnp.arange(token_count, dtype=jnp.int32)
    segment = jnp.sum((token_ids[:, None] >= 4 * slot_ends[None, :]).astype(jnp.int32), axis=1)
    return (patch_rows, is_live, segment)


def owner_ranks(owner_ids, is_live):
    slot_ids = jnp.arange(owner_ids.shape[0], dtype=jnp.int32)
    earlier = (
        (owner_ids[:, None] == owner_ids[None, :])
        & (slot_ids[None, :] < slot_ids[:, None])
        & is_live[None, :]
    )
    return jnp.sum(earlier.astype(jnp.int32), axis=1)


def dest_tokens(patch_rows, is_live, owners, ranks, capacity, devices_req):
    target = jnp.where(is_live, owners * capacity + ranks, -1)
    rows = jnp.arange(devices_req * capacity, dtype=jnp.int32)
    hit = (target[None, :] == rows[:, None]).astype(jnp.int32)
    return jnp.sum(hit[:, :, None] * (patch_rows[None] + 1), axis=1) - 1


def swap(value, axis, bit):
    count = lax.axis_size(axis)
    return lax.ppermute(value, axis, [(i, i ^ bit) for i in range(count)])


def ring(value, step=1):
    count = lax.axis_size("req")
    return lax.ppermute(value, "req", [(i, (i + 2 * step) % count) for i in range(count)])


def call(kernel, name, out, operands, flops, scalars=0, raw=0, scratch=(), ties=()):
    used = len(operands)
    operands = tuple(operands) + tuple(x[:8, :128] for x in ties)
    raw = raw + len(ties)

    def untied(*refs):
        kernel(*refs[:used], *refs[used + len(ties) :])

    def whole(x):
        return pl.BlockSpec(x.shape, lambda i: (0,) * len(x.shape))

    blocks = operands[scalars : len(operands) - raw]
    moved = sum(x.size * x.dtype.itemsize for x in operands[scalars:] + tuple(out))
    return pl.pallas_call(
        untied,
        grid=(1,),
        out_shape=tuple(out),
        in_specs=[pl.BlockSpec(memory_space=pltpu.SMEM)] * scalars
        + [whole(x) for x in blocks]
        + [pl.BlockSpec(memory_space=pl.ANY)] * raw,
        out_specs=tuple(whole(x) for x in out),
        scratch_shapes=scratch,
        compiler_params=pltpu.CompilerParams(vmem_limit_bytes=20 << 20),
        cost_estimate=pl.CostEstimate(flops=flops, bytes_accessed=moved, transcendentals=0),
        name=name,
    )(*operands)


def array(shape, dtype):
    return jax.ShapeDtypeStruct(shape, dtype)


def split_kernel(w_ref, q_ref, k_ref, v_ref):
    for head in range(q_ref.shape[1] // HEAD_DIM):
        to = pl.ds(head * HEAD_DIM, HEAD_DIM)
        for i, ref in enumerate((q_ref, k_ref, v_ref)):
            ref[:, to] = w_ref[:, pl.ds((3 * head + i) * HEAD_DIM, HEAD_DIM)]


def norm_kernel(side_ref, tokens_ref, gain_ref, mine_ref, others_ref):
    rows, width = tokens_ref.shape
    depth = width // 8
    step = 48

    @pl.loop(0, rows // step)
    def _(i):
        at = pl.ds(pl.multiple_of(i * step, step), step)
        values = tokens_ref[at, :].astype(F32)
        inverse = lax.rsqrt(jnp.mean(values * values, axis=1, keepdims=True) + 1e-06)
        normed = values * inverse * gain_ref[...]
        for plane in range(width // (2 * depth)):
            low = normed[:, 2 * plane * depth : (2 * plane + 1) * depth]
            high = normed[:, (2 * plane + 1) * depth : (2 * plane + 2) * depth]
            to = pl.ds(plane * depth, depth)
            mine_ref[at, to] = jnp.where(side_ref[0] == 0, low, high).astype(BF16)
            others_ref[at, to] = jnp.where(side_ref[0] == 0, high, low).astype(BF16)
        filled = mine_ref.shape[1]
        others_ref[at, filled:] = jnp.zeros((step, others_ref.shape[1] - filled), BF16)


def norm_tokens(side, tokens, norm_gain):
    rows, columns = tokens.shape[0], tokens.shape[1] // 2
    out = (array((rows, columns), BF16), array((rows, pl.cdiv(columns, 128) * 128), BF16))
    return call(norm_kernel, "norm_tokens", out, (side, tokens, norm_gain[None]), 0, scalars=1)


def place_blocks(plane, block_refs, weights_ref, sems):
    count, depth = len(block_refs), block_refs[0].shape[0]
    copies = []
    for i, ref in enumerate(block_refs):
        first = lax.rem(plane + count - i, count) * depth
        to = weights_ref.at[pl.ds(pl.multiple_of(first, 16), depth), :]
        copies.append(pltpu.make_async_copy(ref, to, sems.at[i]))
    for copy in copies:
        copy.start()
    for copy in copies:
        copy.wait()


def project_kernel(plane_ref, mine_ref, theirs_ref, *refs):
    *block_refs, own_ref, peer_ref, weights_ref, sems = refs
    place_blocks(plane_ref[0], block_refs, weights_ref, sems)
    weights = weights_ref[...]
    theirs = theirs_ref[:, : weights.shape[0]]
    peer_ref[...] = jnp.dot(theirs, weights, preferred_element_type=F32).astype(BF16)
    own_ref[...] = jnp.dot(mine_ref[...], weights, preferred_element_type=F32)


def project(plane, mine, theirs, blocks):
    rows, columns = mine.shape[0], blocks[0].shape[1]
    depth = blocks[0].shape[0] * len(blocks)
    return call(
        project_kernel,
        "project",
        (array((rows, columns), F32), array((rows, columns), BF16)),
        (plane, mine, theirs, *blocks),
        4 * rows * depth * columns,
        scalars=1,
        raw=len(blocks),
        scratch=(
            pltpu.VMEM((depth, columns), BF16),
            pltpu.SemaphoreType.DMA((len(blocks),)),
        ),
    )


def scores_kernel(q_ref, q_got_ref, k_ref, k_got_ref, q_gain_ref, k_gain_ref, raw_ref, sums_ref):
    share = q_ref.shape[1]
    queries = q_ref[...] + q_got_ref[...].astype(F32)
    key_vecs = k_ref[...] + k_got_ref[...].astype(F32)
    ones = jnp.ones((8, share), F32)
    for i, values in enumerate((queries, key_vecs)):
        totals = lax.dot_general(
            ones,
            values * values,
            (((1,), (1,)), ((), ())),
            precision=lax.Precision.HIGHEST,
            preferred_element_type=F32,
        )
        sums_ref[i : i + 1, :] = totals[0:1]
    queries = queries * (q_gain_ref[...] * (1.0 / math.sqrt(HEAD_DIM)))
    key_vecs = key_vecs * k_gain_ref[...]
    for head in range(raw_ref.shape[0]):
        part = slice(head * HEAD_DIM, (head + 1) * HEAD_DIM)
        raw_ref[head] = lax.dot_general(
            queries[:, part],
            key_vecs[:, part],
            (((1,), (1,)), ((), ())),
            precision=lax.Precision.HIGHEST,
            preferred_element_type=F32,
        )


def attend_kernel(raw_ref, sums_ref, segment_ref, v_ref, v_got_ref, out_ref):
    rows = raw_ref.shape[1]
    scales = lax.rsqrt(sums_ref[...] / (HEADS * HEAD_DIM) + 1e-06)
    q_scale = jnp.broadcast_to(scales[0:1], (128, rows)).T[:, 0:1]
    k_scale = scales[1:2]
    segment = segment_ref[...]
    same = jnp.broadcast_to(segment, (128, rows)).T[:, 0:1] == segment
    values = (v_ref[...] + v_got_ref[...].astype(F32)).astype(BF16)
    for head in range(raw_ref.shape[0]):
        part = slice(head * HEAD_DIM, (head + 1) * HEAD_DIM)
        scores = raw_ref[head] * q_scale * k_scale
        scores = jnp.where(same, scores, -1e30)
        raised = jnp.exp(scores - jnp.max(scores, axis=1, keepdims=True))
        probs = (raised / jnp.sum(raised, axis=1, keepdims=True)).astype(BF16)
        out_ref[:, part] = jnp.dot(
            probs, values[:, part], preferred_element_type=F32
        ).astype(BF16)


def project_out_kernel(place_ref, attended_ref, *refs):
    *block_refs, sent_ref, kept_far_ref, kept_ref, weights_ref, sems = refs
    depth = block_refs[0].shape[0]
    place_blocks(place_ref[0], block_refs, weights_ref, sems)
    column = place_ref[2]
    attended = attended_ref[...]

    def term(index):
        rows = weights_ref[pl.ds(pl.multiple_of(index * depth, 16), depth), :]
        return lax.dot_general(
            rows, attended, (((1,), (1,)), ((), ())), preferred_element_type=F32
        )

    sent_ref[0] = term(column ^ 3).astype(BF16)
    sent_ref[1] = term(column ^ 1).astype(BF16)
    kept_far_ref[...] = term(column ^ 2)
    kept_ref[...] = term(column)


def project_out(place, attended, blocks):
    rows = attended.shape[0]
    depth, width = blocks[0].shape
    kept = array((depth, rows), F32)
    return call(
        project_out_kernel,
        "project_out",
        (array((2, depth, rows), BF16), kept, kept),
        (place, attended, *blocks),
        2 * rows * depth * width * len(blocks),
        scalars=1,
        raw=len(blocks),
        scratch=(
            pltpu.VMEM((depth * len(blocks), width), BF16),
            pltpu.SemaphoreType.DMA((len(blocks),)),
        ),
    )


def far_kernel(kept_ref, near_ref, far_ref):
    far_ref[...] = (kept_ref[...] + near_ref[0].astype(F32)).astype(BF16)


def hidden_of(kept_ref, near_ref, far_ref, token_ref):
    attn_out = kept_ref[...] + near_ref[1].astype(F32) + far_ref[...].astype(F32)
    return (token_ref[...].astype(F32) + attn_out).astype(BF16)


def sum_tokens(hidden, sums_ref, first=0):
    hidden = hidden.astype(F32)
    sums_ref[first : first + 1, :] = jnp.sum(hidden, axis=0, keepdims=True)
    sums_ref[first + 1 : first + 2, :] = jnp.sum(hidden * hidden, axis=0, keepdims=True)


def pack_rows(hidden, chosen_ref, rows_ref, half):
    depth = hidden.shape[0]
    count, _, rows, _ = rows_ref.shape
    for patch in range(4):
        picked = lax.dot_general(
            chosen_ref[pl.ds(patch * rows * count, rows * count), :],
            hidden,
            (((1,), (1,)), ((), ())),
            preferred_element_type=F32,
        )
        picked = picked.reshape(count, rows, depth).astype(BF16)
        rows_ref[:, half, :, pl.ds(patch * depth, depth)] = picked


def first_pack_kernel(kept_ref, near_ref, far_ref, token_ref, chosen_ref, rows_ref, sums_ref):
    hidden = hidden_of(kept_ref, near_ref, far_ref, token_ref)
    pack_rows(hidden, chosen_ref, rows_ref, 0)
    sum_tokens(hidden, sums_ref)


def second_pack_kernel(
    first_ref, first_sums_ref, kept_ref, near_ref, far_ref, token_ref, chosen_ref,
    rows_ref, sums_ref,
):
    hidden = hidden_of(kept_ref, near_ref, far_ref, token_ref)
    rows_ref[:, 0] = first_ref[:, 0]
    pack_rows(hidden, chosen_ref, rows_ref, 1)
    sums_ref[0:2, :] = first_sums_ref[...]
    sum_tokens(hidden, sums_ref, 2)


def finish_kernel(stats_ref, gain_ref, bias_ref, rows_ref, out_ref):
    count, _, rows, _ = rows_ref.shape
    depth = out_ref.shape[2] // 2
    for i in range(count):
        to = pl.ds(i * rows, rows)
        scale, shift, live = (stats_ref[j, to][:, 0:1] for j in range(3))
        for patch in range(4):
            part = slice(patch * depth, (patch + 1) * depth)
            parts = [rows_ref[i, 0, :, part].astype(F32), rows_ref[i ^ 1, 1, :, part].astype(F32)]
            values = jnp.concatenate(parts[::-1] if i % 2 else parts, axis=1)
            gain, bias = gain_ref[patch : patch + 1, :], bias_ref[patch : patch + 1, :]
            values = (values * scale + shift) * gain + live * bias
            out_ref[to, patch, :] = values.astype(BF16)


def finish(stats, proj_gain, proj_bias, arrived):
    rows = stats.shape[1]
    stats = jnp.broadcast_to(stats[:, :, None], (3, rows, 128))
    out = array((rows,) + proj_gain.shape, BF16)
    operands = (stats, proj_gain, proj_bias, arrived)
    return call(finish_kernel, "finish", (out,), operands, 6 * out.size)[0]


def after(value, *first):
    return lax.optimization_barrier((value,) + first)[0]


def general_body(tokens, norm_gain, w_qkv, q_gain, k_gain, w_out, grids, owners, proj_gain, proj_bias):
    token_count = tokens.shape[0]
    slot_count = owners.shape[0]
    quarter = proj_gain.shape[1]
    head_share = q_gain.shape[0]
    head_count = head_share // HEAD_DIM
    head_width = HEADS * HEAD_DIM
    score_scale = 1.0 / math.sqrt(HEAD_DIM)
    feature_total = 4 * D
    devices_req = lax.axis_size("req")
    capacity = max(2, (2 * slot_count + devices_req - 1) // devices_req)
    patch_rows, is_live, segment = merge_layout(grids, token_count, slot_count)
    token_float = tokens.astype(jnp.float32)
    mean_square = jnp.mean(token_float * token_float, axis=1, keepdims=True)
    normed = (token_float * lax.rsqrt(mean_square + 1e-06) * norm_gain).astype(jnp.bfloat16)
    projected = jnp.dot(
        normed, lax.all_gather(w_qkv, "req", axis=0, tiled=True), preferred_element_type=jnp.float32
    )
    projected = projected.reshape(token_count, head_count, 3, HEAD_DIM)
    queries = projected[:, :, 0]
    key_vecs = projected[:, :, 1]
    values = projected[:, :, 2].astype(jnp.bfloat16)
    q_gains = q_gain.reshape(head_count, HEAD_DIM)
    k_gains = k_gain.reshape(head_count, HEAD_DIM)
    local_q = jnp.sum(queries * queries, axis=(1, 2))
    local_k = jnp.sum(key_vecs * key_vecs, axis=(1, 2))
    q_total, k_total = lax.psum((local_q, local_k), "tp")
    q_scale = lax.rsqrt(q_total / head_width + 1e-06)
    k_scale = lax.rsqrt(k_total / head_width + 1e-06)
    q_normed = queries * q_scale[:, None, None] * q_gains
    k_normed = key_vecs * k_scale[:, None, None] * k_gains
    scores = (
        jnp.einsum("qhd,khd->hqk", q_normed, k_normed, precision=lax.Precision.HIGHEST)
        * score_scale
    )
    same_image = segment[:, None] == segment[None, :]
    scores = jnp.where(same_image[None], scores, -1e30)
    row_top = jnp.max(scores, axis=2, keepdims=True)
    weights_raw = jnp.exp(scores - row_top)
    probs = (weights_raw / jnp.sum(weights_raw, axis=2, keepdims=True)).astype(jnp.bfloat16)
    attended = jnp.einsum("hqk,khd->qhd", probs, values, preferred_element_type=jnp.float32)
    attended = attended.astype(jnp.bfloat16).reshape(token_count, head_share)
    partial_sum = jnp.dot(
        attended,
        lax.all_gather(w_out, "req", axis=1, tiled=True),
        preferred_element_type=jnp.float32,
    )
    mine = lax.psum_scatter(
        partial_sum.astype(jnp.bfloat16), "tp", scatter_dimension=1, tiled=True
    ).astype(jnp.float32)
    token_mine = lax.dynamic_slice_in_dim(token_float, lax.axis_index("tp") * quarter, quarter, 1)
    hidden = (token_mine + mine).astype(jnp.bfloat16)
    merged = jnp.where(is_live[:, None, None], hidden[patch_rows], jnp.zeros((), jnp.bfloat16))
    ranks = owner_ranks(owners, is_live)
    target_owner = jnp.where(is_live, owners, devices_req)
    send_slots = jnp.zeros((devices_req, capacity, 4, quarter), jnp.bfloat16)
    send_slots = send_slots.at[target_owner, ranks].set(merged, mode="drop")
    owner_ids = jnp.arange(devices_req, dtype=jnp.int32)
    dest_counts = jnp.sum(
        ((owners[None, :] == owner_ids[:, None]) & is_live[None, :]).astype(jnp.int32), axis=1
    )
    dest_counts = dest_counts[:, None]
    arrived, source_counts = (
        lax.all_to_all(send_slots, "req", split_axis=0, concat_axis=0, tiled=True),
        lax.all_to_all(dest_counts, "req", split_axis=0, concat_axis=0, tiled=True),
    )
    slot_live = jnp.arange(capacity, dtype=jnp.int32)[None, :] < source_counts
    arrived_float = arrived.astype(jnp.float32)
    row_sum = jnp.sum(arrived_float, axis=(2, 3))
    row_sq = jnp.sum(arrived_float * arrived_float, axis=(2, 3))
    row_sum, row_sq = lax.psum((row_sum, row_sq), "tp")
    mean_value = row_sum / feature_total
    variance = row_sq / feature_total - mean_value * mean_value
    normed_out = (arrived_float - mean_value[:, :, None, None]) * lax.rsqrt(variance + 1e-05)[
        :, :, None, None
    ] * proj_gain + proj_bias
    normed_out = jnp.where(slot_live[:, :, None, None], normed_out, 0.0).astype(jnp.bfloat16)
    result = normed_out.reshape(devices_req * capacity, 4, quarter)
    return result


def body(tokens, norm_gain, w_qkv, q_gain, k_gain, w_out, grids, owners, proj_gain, proj_bias):
    token_count = tokens.shape[0]
    slot_count = owners.shape[0]
    quarter = proj_gain.shape[1]
    head_share = q_gain.shape[0]
    head_count = head_share // HEAD_DIM
    feature_total = 4 * D
    devices_req = lax.axis_size("req")
    planes = devices_req // 2
    capacity = max(2, (2 * slot_count + devices_req - 1) // devices_req)
    me = lax.axis_index("req")
    plane, side = me // 2, me % 2
    column = lax.axis_index("tp")
    token_ids = jnp.arange(token_count, dtype=jnp.int32)

    part = array((w_qkv.shape[0], head_share), BF16)
    w_q, w_k, w_v = call(split_kernel, "split_heads", (part,) * 3, (w_qkv,), 0)
    w_o = w_out.T
    q_up, q_down, k_up = ring(w_q), ring(w_q, -1), ring(w_k)
    k_down = ring(after(w_k, q_up), -1)
    q_far = ring(after(q_up, q_down))
    k_far = ring(k_up)
    v_up = ring(after(w_v, k_down))
    v_down = ring(after(w_v, q_far), -1)
    v_far = ring(v_up)
    q_blocks, k_blocks = [w_q, q_up, q_far, q_down], [w_k, k_up, k_far, k_down]
    v_blocks = [w_v, v_up, v_far, v_down]

    places = jnp.stack([plane, side, column]).astype(jnp.int32)
    mine, others = norm_tokens(places[1:2], after(tokens, w_q), norm_gain)
    theirs = swap(others, "req", 1)

    own_routes = after(jnp.concatenate([owners, grids.reshape(-1)]), k_down)
    chosen, in_row = [], []
    for routes in (own_routes, swap(own_routes, "req", 1)):
        owner_ids, grid = routes[:slot_count], routes[slot_count:].reshape(-1, 2)
        patch_rows, is_live, tokens_of = merge_layout(grid, token_count, slot_count)
        ranks = owner_ranks(owner_ids, is_live)
        row_tokens = dest_tokens(
            patch_rows, is_live, owner_ids, ranks, capacity, devices_req
        )
        picks = row_tokens.T.reshape(-1)[:, None] == token_ids[None, :]
        chosen.append(picks.astype(BF16))
        picks = row_tokens[:, :, None] == token_ids[None, None, :]
        in_row.append(jnp.any(picks, axis=1).astype(F32))
        if routes is own_routes:
            segment, row_live = tokens_of, (row_tokens[:, 0] >= 0).astype(F32)
    token_mine = lax.dynamic_slice_in_dim(after(tokens, k_down), column * quarter, quarter, 1).T
    token_mine = token_mine.reshape(2, quarter // 2, token_count)
    token_parts = [
        lax.dynamic_index_in_dim(token_mine, side, 0, keepdims=False),
        swap(lax.dynamic_index_in_dim(token_mine, 1 - side, 0, keepdims=False), "req", 1),
    ]

    mine = after(mine, *token_parts, *chosen)
    queries, q_peer = project(places[0:1], mine, theirs, q_blocks)
    q_got = swap(q_peer, "req", 1)
    key_vecs, k_peer = project(places[0:1], mine, theirs, k_blocks)
    k_got = swap(k_peer, "req", 1)
    o_up, o_down = ring(after(w_o, v_up, q_peer)), ring(after(w_o, v_down, k_peer), -1)
    o_blocks = [w_o, o_up, ring(o_up), o_down]
    values, v_peer = project(places[0:1], mine, theirs, v_blocks)
    v_got = swap(v_peer, "req", 1)
    raw, sums = call(
        scores_kernel,
        "scores",
        (
            array((head_count, token_count, token_count), F32),
            array((2, token_count), F32),
        ),
        (queries, q_got, key_vecs, k_got, q_gain[None], k_gain[None]),
        12 * token_count * token_count * head_share,
        ties=(v_peer,),
    )
    (attended,) = call(
        attend_kernel,
        "attend",
        (array((token_count, head_share), BF16),),
        (raw, lax.psum(sums, "tp"), segment.astype(F32)[None], values, v_got),
        2 * token_count * token_count * head_share,
    )

    parts = []
    for heads_out, token_part in zip((attended, swap(attended, "req", 1)), token_parts):
        sent, kept_far, kept = project_out(places, heads_out, o_blocks)
        near = swap(sent, "tp", 1)
        (far,) = call(far_kernel, "far_sum", (array(kept.shape, BF16),), (kept_far, near), 0)
        parts.append((kept, near, swap(far, "tp", 2), token_part))
    packed = array((devices_req, 2, capacity, 2 * quarter), BF16)
    flops = 2 * chosen[0].size * quarter
    first_rows, own_sums = call(
        first_pack_kernel,
        "first_pack",
        (packed, array((2, token_count), F32)),
        (*parts[0], chosen[0]),
        flops,
    )
    rows, token_sums = call(
        second_pack_kernel,
        "second_pack",
        (packed, array((4, token_count), F32)),
        (first_rows, own_sums, *parts[1], chosen[1]),
        flops,
    )
    arrived = lax.all_to_all(rows, "req", split_axis=0, concat_axis=0, tiled=True)

    token_sums = lax.psum(token_sums, "tp").reshape(2, 2, token_count)
    own_sums, next_sums = (
        jnp.sum(picks[None] * sums[:, None, :], axis=2) for picks, sums in zip(in_row, token_sums)
    )
    got = swap(next_sums, "req", 1)
    row_sums = (own_sums + got) / feature_total
    mean_value = row_sums[0]
    inverse = lax.rsqrt(row_sums[1] - mean_value * mean_value + 1e-05) * row_live
    stats = jnp.stack([inverse, -mean_value * inverse, row_live])
    stats = stats.reshape(3, 1, devices_req, capacity)
    bit = 1
    while bit < devices_req:
        got = swap(stats, "req", bit)
        lower = (me & bit) == 0
        stats = jnp.concatenate(
            [jnp.where(lower, stats, got), jnp.where(lower, got, stats)], axis=1
        )
        bit *= 2
    stats = lax.dynamic_index_in_dim(stats, me, 2, keepdims=False)
    stats = stats.reshape(3, devices_req * capacity)
    return finish(stats, proj_gain, proj_bias, arrived)


def solution(mesh):
    placed = (
        P("req", None),
        P(),
        P("req", "tp"),
        P("tp"),
        P("tp"),
        P("tp", "req"),
        P("req", None),
        P("req"),
        P(None, "tp"),
        P(None, "tp"),
    )
    planes, odd = divmod(mesh.shape["req"], 2)
    fits = not odd and planes == mesh.shape["tp"] == 4
    return jax.shard_map(
        body if fits else general_body, mesh=mesh, in_specs=placed, out_specs=P("req", None, "tp"), check_vma=False
    )
```

```python
import math

import jax
import jax.numpy as jnp
from jax import lax
from jax.experimental import pallas as pl
from jax.experimental.pallas import tpu as pltpu
from jax.sharding import PartitionSpec as P

D = 3200
HEADS = 16
HEAD_DIM = 128
BF16 = jnp.bfloat16
F32 = jnp.float32


def merge_layout(grid, token_count, slot_count):
    half_rows = grid[:, 0]
    half_cols = grid[:, 1]
    image_slots = half_rows * half_cols
    slot_ends = jnp.cumsum(image_slots)
    slot_starts = slot_ends - image_slots
    slot_ids = jnp.arange(slot_count, dtype=jnp.int32)
    image_ids = jnp.sum((slot_ids[:, None] >= slot_ends[None, :]).astype(jnp.int32), axis=1)
    image_count = grid.shape[0]
    is_live = image_ids < image_count
    one_hot = (image_ids[:, None] == jnp.arange(image_count, dtype=jnp.int32)[None, :]).astype(
        jnp.int32
    )
    cols_here = jnp.maximum(jnp.sum(one_hot * half_cols[None, :], axis=1), 1)
    start_here = jnp.sum(one_hot * slot_starts[None, :], axis=1)
    offset = slot_ids - start_here
    row_half = offset // cols_here
    col_half = offset % cols_here
    first_row = 4 * start_here + 4 * row_half * cols_here + 2 * col_half
    patch_rows = jnp.stack(
        [first_row, first_row + 1, first_row + 2 * cols_here, first_row + 2 * cols_here + 1], axis=1
    )
    patch_rows = jnp.where(is_live[:, None], patch_rows, 0)
    token_ids = jnp.arange(token_count, dtype=jnp.int32)
    segment = jnp.sum((token_ids[:, None] >= 4 * slot_ends[None, :]).astype(jnp.int32), axis=1)
    return (patch_rows, is_live, segment)


def owner_ranks(owner_ids, is_live):
    slot_ids = jnp.arange(owner_ids.shape[0], dtype=jnp.int32)
    earlier = (
        (owner_ids[:, None] == owner_ids[None, :])
        & (slot_ids[None, :] < slot_ids[:, None])
        & is_live[None, :]
    )
    return jnp.sum(earlier.astype(jnp.int32), axis=1)


def dest_tokens(patch_rows, is_live, owners, ranks, capacity, devices_req):
    target = jnp.where(is_live, owners * capacity + ranks, -1)
    rows = jnp.arange(devices_req * capacity, dtype=jnp.int32)
    hit = (target[None, :] == rows[:, None]).astype(jnp.int32)
    return jnp.sum(hit[:, :, None] * (patch_rows[None] + 1), axis=1) - 1


def swap(value, axis, bit):
    count = lax.axis_size(axis)
    return lax.ppermute(value, axis, [(i, i ^ bit) for i in range(count)])


def ring(value, step=1):
    count = lax.axis_size("req")
    return lax.ppermute(value, "req", [(i, (i + 2 * step) % count) for i in range(count)])


def call(kernel, name, out, operands, flops, scalars=0, raw=0, scratch=(), ties=()):
    used = len(operands)
    operands = tuple(operands) + tuple(x[:8, :128] for x in ties)
    raw = raw + len(ties)

    def untied(*refs):
        kernel(*refs[:used], *refs[used + len(ties) :])

    def whole(x):
        return pl.BlockSpec(x.shape, lambda i: (0,) * len(x.shape))

    blocks = operands[scalars : len(operands) - raw]
    moved = sum(x.size * x.dtype.itemsize for x in operands[scalars:] + tuple(out))
    return pl.pallas_call(
        untied,
        grid=(1,),
        out_shape=tuple(out),
        in_specs=[pl.BlockSpec(memory_space=pltpu.SMEM)] * scalars
        + [whole(x) for x in blocks]
        + [pl.BlockSpec(memory_space=pl.ANY)] * raw,
        out_specs=tuple(whole(x) for x in out),
        scratch_shapes=scratch,
        compiler_params=pltpu.CompilerParams(vmem_limit_bytes=20 << 20),
        cost_estimate=pl.CostEstimate(flops=flops, bytes_accessed=moved, transcendentals=0),
        name=name,
    )(*operands)


def array(shape, dtype):
    return jax.ShapeDtypeStruct(shape, dtype)


def split_kernel(w_ref, q_ref, k_ref, v_ref):
    for head in range(q_ref.shape[1] // HEAD_DIM):
        to = pl.ds(head * HEAD_DIM, HEAD_DIM)
        for i, ref in enumerate((q_ref, k_ref, v_ref)):
            ref[:, to] = w_ref[:, pl.ds((3 * head + i) * HEAD_DIM, HEAD_DIM)]


def norm_kernel(side_ref, tokens_ref, gain_ref, mine_ref, others_ref):
    rows, width = tokens_ref.shape
    depth = width // 8
    step = 48

    @pl.loop(0, rows // step)
    def _(i):
        at = pl.ds(pl.multiple_of(i * step, step), step)
        values = tokens_ref[at, :].astype(F32)
        inverse = lax.rsqrt(jnp.mean(values * values, axis=1, keepdims=True) + 1e-06)
        normed = values * inverse * gain_ref[...]
        for plane in range(width // (2 * depth)):
            low = normed[:, 2 * plane * depth : (2 * plane + 1) * depth]
            high = normed[:, (2 * plane + 1) * depth : (2 * plane + 2) * depth]
            to = pl.ds(plane * depth, depth)
            mine_ref[at, to] = jnp.where(side_ref[0] == 0, low, high).astype(BF16)
            others_ref[at, to] = jnp.where(side_ref[0] == 0, high, low).astype(BF16)
        filled = mine_ref.shape[1]
        others_ref[at, filled:] = jnp.zeros((step, others_ref.shape[1] - filled), BF16)


def norm_tokens(side, tokens, norm_gain):
    rows, columns = tokens.shape[0], tokens.shape[1] // 2
    out = (array((rows, columns), BF16), array((rows, pl.cdiv(columns, 128) * 128), BF16))
    return call(norm_kernel, "norm_tokens", out, (side, tokens, norm_gain[None]), 0, scalars=1)


def place_blocks(plane, block_refs, weights_ref, sems):
    count, depth = len(block_refs), block_refs[0].shape[0]
    copies = []
    for i, ref in enumerate(block_refs):
        first = lax.rem(plane + count - i, count) * depth
        to = weights_ref.at[pl.ds(pl.multiple_of(first, 16), depth), :]
        copies.append(pltpu.make_async_copy(ref, to, sems.at[i]))
    for copy in copies:
        copy.start()
    for copy in copies:
        copy.wait()


def project_kernel(plane_ref, mine_ref, theirs_ref, *refs):
    *block_refs, own_ref, peer_ref, weights_ref, sems = refs
    place_blocks(plane_ref[0], block_refs, weights_ref, sems)
    weights = weights_ref[...]
    theirs = theirs_ref[:, : weights.shape[0]]
    peer_ref[...] = jnp.dot(theirs, weights, preferred_element_type=F32).astype(BF16)
    own_ref[...] = jnp.dot(mine_ref[...], weights, preferred_element_type=F32)


def project(plane, mine, theirs, blocks):
    rows, columns = mine.shape[0], blocks[0].shape[1]
    depth = blocks[0].shape[0] * len(blocks)
    return call(
        project_kernel,
        "project",
        (array((rows, columns), F32), array((rows, columns), BF16)),
        (plane, mine, theirs, *blocks),
        4 * rows * depth * columns,
        scalars=1,
        raw=len(blocks),
        scratch=(
            pltpu.VMEM((depth, columns), BF16),
            pltpu.SemaphoreType.DMA((len(blocks),)),
        ),
    )


def scores_kernel(q_ref, q_got_ref, k_ref, k_got_ref, q_gain_ref, k_gain_ref, raw_ref, sums_ref):
    share = q_ref.shape[1]
    queries = q_ref[...] + q_got_ref[...].astype(F32)
    key_vecs = k_ref[...] + k_got_ref[...].astype(F32)
    ones = jnp.ones((8, share), F32)
    for i, values in enumerate((queries, key_vecs)):
        totals = lax.dot_general(
            ones,
            values * values,
            (((1,), (1,)), ((), ())),
            precision=lax.Precision.HIGHEST,
            preferred_element_type=F32,
        )
        sums_ref[i : i + 1, :] = totals[0:1]
    queries = queries * (q_gain_ref[...] * (1.0 / math.sqrt(HEAD_DIM)))
    key_vecs = key_vecs * k_gain_ref[...]
    for head in range(raw_ref.shape[0]):
        part = slice(head * HEAD_DIM, (head + 1) * HEAD_DIM)
        raw_ref[head] = lax.dot_general(
            queries[:, part],
            key_vecs[:, part],
            (((1,), (1,)), ((), ())),
            precision=lax.Precision.HIGHEST,
            preferred_element_type=F32,
        )


def attend_kernel(raw_ref, sums_ref, segment_ref, v_ref, v_got_ref, out_ref):
    rows = raw_ref.shape[1]
    scales = lax.rsqrt(sums_ref[...] / (HEADS * HEAD_DIM) + 1e-06)
    q_scale = jnp.broadcast_to(scales[0:1], (128, rows)).T[:, 0:1]
    k_scale = scales[1:2]
    segment = segment_ref[...]
    same = jnp.broadcast_to(segment, (128, rows)).T[:, 0:1] == segment
    values = (v_ref[...] + v_got_ref[...].astype(F32)).astype(BF16)
    for head in range(raw_ref.shape[0]):
        part = slice(head * HEAD_DIM, (head + 1) * HEAD_DIM)
        scores = raw_ref[head] * q_scale * k_scale
        scores = jnp.where(same, scores, -1e30)
        raised = jnp.exp(scores - jnp.max(scores, axis=1, keepdims=True))
        probs = (raised / jnp.sum(raised, axis=1, keepdims=True)).astype(BF16)
        out_ref[:, part] = jnp.dot(
            probs, values[:, part], preferred_element_type=F32
        ).astype(BF16)


def project_out_kernel(place_ref, attended_ref, *refs):
    *block_refs, sent_ref, kept_far_ref, kept_ref, weights_ref, sems = refs
    depth = block_refs[0].shape[0]
    place_blocks(place_ref[0], block_refs, weights_ref, sems)
    column = place_ref[2]
    attended = attended_ref[...]

    def term(index):
        rows = weights_ref[pl.ds(pl.multiple_of(index * depth, 16), depth), :]
        return lax.dot_general(
            rows, attended, (((1,), (1,)), ((), ())), preferred_element_type=F32
        )

    sent_ref[0] = term(column ^ 3).astype(BF16)
    sent_ref[1] = term(column ^ 1).astype(BF16)
    kept_far_ref[...] = term(column ^ 2)
    kept_ref[...] = term(column)


def project_out(place, attended, blocks):
    rows = attended.shape[0]
    depth, width = blocks[0].shape
    kept = array((depth, rows), F32)
    return call(
        project_out_kernel,
        "project_out",
        (array((2, depth, rows), BF16), kept, kept),
        (place, attended, *blocks),
        2 * rows * depth * width * len(blocks),
        scalars=1,
        raw=len(blocks),
        scratch=(
            pltpu.VMEM((depth * len(blocks), width), BF16),
            pltpu.SemaphoreType.DMA((len(blocks),)),
        ),
    )


def far_kernel(kept_ref, near_ref, far_ref):
    far_ref[...] = (kept_ref[...] + near_ref[0].astype(F32)).astype(BF16)


def hidden_of(kept_ref, near_ref, far_ref, token_ref):
    attn_out = kept_ref[...] + near_ref[1].astype(F32) + far_ref[...].astype(F32)
    return (token_ref[...].astype(F32) + attn_out).astype(BF16)


def sum_tokens(hidden, sums_ref, first=0):
    hidden = hidden.astype(F32)
    sums_ref[first : first + 1, :] = jnp.sum(hidden, axis=0, keepdims=True)
    sums_ref[first + 1 : first + 2, :] = jnp.sum(hidden * hidden, axis=0, keepdims=True)


def pack_rows(hidden, chosen_ref, rows_ref, half):
    depth = hidden.shape[0]
    count, _, rows, _ = rows_ref.shape
    for patch in range(4):
        picked = lax.dot_general(
            chosen_ref[pl.ds(patch * rows * count, rows * count), :],
            hidden,
            (((1,), (1,)), ((), ())),
            preferred_element_type=F32,
        )
        picked = picked.reshape(count, rows, depth).astype(BF16)
        rows_ref[:, half, :, pl.ds(patch * depth, depth)] = picked


def first_pack_kernel(kept_ref, near_ref, far_ref, token_ref, chosen_ref, rows_ref, sums_ref):
    hidden = hidden_of(kept_ref, near_ref, far_ref, token_ref)
    pack_rows(hidden, chosen_ref, rows_ref, 0)
    sum_tokens(hidden, sums_ref)


def second_pack_kernel(
    first_ref, first_sums_ref, kept_ref, near_ref, far_ref, token_ref, chosen_ref,
    rows_ref, sums_ref,
):
    hidden = hidden_of(kept_ref, near_ref, far_ref, token_ref)
    rows_ref[:, 0] = first_ref[:, 0]
    pack_rows(hidden, chosen_ref, rows_ref, 1)
    sums_ref[0:2, :] = first_sums_ref[...]
    sum_tokens(hidden, sums_ref, 2)


def finish_kernel(plane_ref, stats_ref, gain_ref, bias_ref, rows_ref, out_ref):
    count, _, rows, _ = rows_ref.shape
    depth = out_ref.shape[2] // 2
    for i in range(count):
        to = pl.ds(i * rows, rows)
        place = pl.ds(((plane_ref[0] ^ (i // 2)) * 2 + i % 2) * rows, rows)
        scale, shift, live = (stats_ref[j, place][:, 0:1] for j in range(3))
        for patch in range(4):
            part = slice(patch * depth, (patch + 1) * depth)
            parts = [rows_ref[i, 0, :, part].astype(F32), rows_ref[i ^ 1, 1, :, part].astype(F32)]
            values = jnp.concatenate(parts[::-1] if i % 2 else parts, axis=1)
            gain, bias = gain_ref[patch : patch + 1, :], bias_ref[patch : patch + 1, :]
            values = (values * scale + shift) * gain + live * bias
            out_ref[to, patch, :] = values.astype(BF16)


def finish(plane, stats, proj_gain, proj_bias, arrived):
    rows = stats.shape[1]
    stats = jnp.broadcast_to(stats[:, :, None], (3, rows, 128))
    out = array((rows,) + proj_gain.shape, BF16)
    operands = (plane.reshape(1), stats, proj_gain, proj_bias, arrived)
    return call(finish_kernel, "finish", (out,), operands, 6 * out.size, scalars=1)[0]


def after(value, *first):
    return lax.optimization_barrier((value,) + first)[0]


def general_body(tokens, norm_gain, w_qkv, q_gain, k_gain, w_out, grids, owners, proj_gain, proj_bias):
    token_count = tokens.shape[0]
    slot_count = owners.shape[0]
    quarter = proj_gain.shape[1]
    head_share = q_gain.shape[0]
    head_count = head_share // HEAD_DIM
    head_width = HEADS * HEAD_DIM
    score_scale = 1.0 / math.sqrt(HEAD_DIM)
    feature_total = 4 * D
    devices_req = lax.axis_size("req")
    capacity = max(2, (2 * slot_count + devices_req - 1) // devices_req)
    patch_rows, is_live, segment = merge_layout(grids, token_count, slot_count)
    token_float = tokens.astype(jnp.float32)
    mean_square = jnp.mean(token_float * token_float, axis=1, keepdims=True)
    normed = (token_float * lax.rsqrt(mean_square + 1e-06) * norm_gain).astype(jnp.bfloat16)
    projected = jnp.dot(
        normed, lax.all_gather(w_qkv, "req", axis=0, tiled=True), preferred_element_type=jnp.float32
    )
    projected = projected.reshape(token_count, head_count, 3, HEAD_DIM)
    queries = projected[:, :, 0]
    key_vecs = projected[:, :, 1]
    values = projected[:, :, 2].astype(jnp.bfloat16)
    q_gains = q_gain.reshape(head_count, HEAD_DIM)
    k_gains = k_gain.reshape(head_count, HEAD_DIM)
    local_q = jnp.sum(queries * queries, axis=(1, 2))
    local_k = jnp.sum(key_vecs * key_vecs, axis=(1, 2))
    q_total, k_total = lax.psum((local_q, local_k), "tp")
    q_scale = lax.rsqrt(q_total / head_width + 1e-06)
    k_scale = lax.rsqrt(k_total / head_width + 1e-06)
    q_normed = queries * q_scale[:, None, None] * q_gains
    k_normed = key_vecs * k_scale[:, None, None] * k_gains
    scores = (
        jnp.einsum("qhd,khd->hqk", q_normed, k_normed, precision=lax.Precision.HIGHEST)
        * score_scale
    )
    same_image = segment[:, None] == segment[None, :]
    scores = jnp.where(same_image[None], scores, -1e30)
    row_top = jnp.max(scores, axis=2, keepdims=True)
    weights_raw = jnp.exp(scores - row_top)
    probs = (weights_raw / jnp.sum(weights_raw, axis=2, keepdims=True)).astype(jnp.bfloat16)
    attended = jnp.einsum("hqk,khd->qhd", probs, values, preferred_element_type=jnp.float32)
    attended = attended.astype(jnp.bfloat16).reshape(token_count, head_share)
    partial_sum = jnp.dot(
        attended,
        lax.all_gather(w_out, "req", axis=1, tiled=True),
        preferred_element_type=jnp.float32,
    )
    mine = lax.psum_scatter(
        partial_sum.astype(jnp.bfloat16), "tp", scatter_dimension=1, tiled=True
    ).astype(jnp.float32)
    token_mine = lax.dynamic_slice_in_dim(token_float, lax.axis_index("tp") * quarter, quarter, 1)
    hidden = (token_mine + mine).astype(jnp.bfloat16)
    merged = jnp.where(is_live[:, None, None], hidden[patch_rows], jnp.zeros((), jnp.bfloat16))
    ranks = owner_ranks(owners, is_live)
    target_owner = jnp.where(is_live, owners, devices_req)
    send_slots = jnp.zeros((devices_req, capacity, 4, quarter), jnp.bfloat16)
    send_slots = send_slots.at[target_owner, ranks].set(merged, mode="drop")
    owner_ids = jnp.arange(devices_req, dtype=jnp.int32)
    dest_counts = jnp.sum(
        ((owners[None, :] == owner_ids[:, None]) & is_live[None, :]).astype(jnp.int32), axis=1
    )
    dest_counts = dest_counts[:, None]
    arrived, source_counts = (
        lax.all_to_all(send_slots, "req", split_axis=0, concat_axis=0, tiled=True),
        lax.all_to_all(dest_counts, "req", split_axis=0, concat_axis=0, tiled=True),
    )
    slot_live = jnp.arange(capacity, dtype=jnp.int32)[None, :] < source_counts
    arrived_float = arrived.astype(jnp.float32)
    row_sum = jnp.sum(arrived_float, axis=(2, 3))
    row_sq = jnp.sum(arrived_float * arrived_float, axis=(2, 3))
    row_sum, row_sq = lax.psum((row_sum, row_sq), "tp")
    mean_value = row_sum / feature_total
    variance = row_sq / feature_total - mean_value * mean_value
    normed_out = (arrived_float - mean_value[:, :, None, None]) * lax.rsqrt(variance + 1e-05)[
        :, :, None, None
    ] * proj_gain + proj_bias
    normed_out = jnp.where(slot_live[:, :, None, None], normed_out, 0.0).astype(jnp.bfloat16)
    result = normed_out.reshape(devices_req * capacity, 4, quarter)
    return result


def body(tokens, norm_gain, w_qkv, q_gain, k_gain, w_out, grids, owners, proj_gain, proj_bias):
    token_count = tokens.shape[0]
    slot_count = owners.shape[0]
    quarter = proj_gain.shape[1]
    head_share = q_gain.shape[0]
    head_count = head_share // HEAD_DIM
    feature_total = 4 * D
    devices_req = lax.axis_size("req")
    planes = devices_req // 2
    capacity = max(2, (2 * slot_count + devices_req - 1) // devices_req)
    me = lax.axis_index("req")
    plane, side = me // 2, me % 2
    column = lax.axis_index("tp")
    token_ids = jnp.arange(token_count, dtype=jnp.int32)

    part = array((w_qkv.shape[0], head_share), BF16)
    w_q, w_k, w_v = call(split_kernel, "split_heads", (part,) * 3, (w_qkv,), 0)
    w_o = w_out.T
    q_up, q_down, k_up = ring(w_q), ring(w_q, -1), ring(w_k)
    k_down = ring(after(w_k, q_up), -1)
    q_far = ring(after(q_up, q_down))
    k_far = ring(k_up)
    v_up = ring(after(w_v, q_far))
    v_down = ring(after(w_v, k_far), -1)
    v_far = ring(v_up)
    q_blocks, k_blocks = [w_q, q_up, q_far, q_down], [w_k, k_up, k_far, k_down]
    v_blocks = [w_v, v_up, v_far, v_down]

    places = jnp.stack([plane, side, column]).astype(jnp.int32)
    mine, others = norm_tokens(places[1:2], after(tokens, w_q), norm_gain)
    theirs = swap(others, "req", 1)

    own_routes = after(jnp.concatenate([owners, grids.reshape(-1)]), k_down)
    chosen, in_row = [], []
    for routes in (own_routes, swap(own_routes, "req", 1)):
        owner_ids, grid = routes[:slot_count], routes[slot_count:].reshape(-1, 2)
        patch_rows, is_live, tokens_of = merge_layout(grid, token_count, slot_count)
        ranks = owner_ranks(owner_ids, is_live)
        row_tokens = dest_tokens(
            patch_rows, is_live, owner_ids, ranks, capacity, devices_req
        )
        picks = row_tokens.T.reshape(-1)[:, None] == token_ids[None, :]
        chosen.append(picks.astype(BF16))
        picks = row_tokens[:, :, None] == token_ids[None, None, :]
        in_row.append(jnp.any(picks, axis=1).astype(F32))
        if routes is own_routes:
            segment, row_live = tokens_of, (row_tokens[:, 0] >= 0).astype(F32)
    token_mine = lax.dynamic_slice_in_dim(after(tokens, k_down), column * quarter, quarter, 1).T
    token_mine = token_mine.reshape(2, quarter // 2, token_count)
    token_parts = [
        lax.dynamic_index_in_dim(token_mine, side, 0, keepdims=False),
        swap(lax.dynamic_index_in_dim(token_mine, 1 - side, 0, keepdims=False), "req", 1),
    ]

    mine = after(mine, *token_parts, *chosen)
    queries, q_peer = project(places[0:1], mine, theirs, q_blocks)
    q_got = swap(q_peer, "req", 1)
    key_vecs, k_peer = project(places[0:1], mine, theirs, k_blocks)
    k_got = swap(k_peer, "req", 1)
    o_up, o_down = ring(after(w_o, v_up, q_peer)), ring(after(w_o, v_down, k_peer), -1)
    o_blocks = [w_o, o_up, ring(o_up), o_down]
    values, v_peer = project(places[0:1], mine, theirs, v_blocks)
    v_got = swap(v_peer, "req", 1)
    raw, sums = call(
        scores_kernel,
        "scores",
        (
            array((head_count, token_count, token_count), F32),
            array((2, token_count), F32),
        ),
        (queries, q_got, key_vecs, k_got, q_gain[None], k_gain[None]),
        12 * token_count * token_count * head_share,
        ties=(v_peer,),
    )
    (attended,) = call(
        attend_kernel,
        "attend",
        (array((token_count, head_share), BF16),),
        (raw, lax.psum(sums, "tp"), segment.astype(F32)[None], values, v_got),
        2 * token_count * token_count * head_share,
    )

    parts = []
    for heads_out, token_part in zip((attended, swap(attended, "req", 1)), token_parts):
        sent, kept_far, kept = project_out(places, heads_out, o_blocks)
        near = swap(sent, "tp", 1)
        (far,) = call(far_kernel, "far_sum", (array(kept.shape, BF16),), (kept_far, near), 0)
        parts.append((kept, near, swap(far, "tp", 2), token_part))
    packed = array((devices_req, 2, capacity, 2 * quarter), BF16)
    flops = 2 * chosen[0].size * quarter
    first_rows, own_sums = call(
        first_pack_kernel,
        "first_pack",
        (packed, array((2, token_count), F32)),
        (*parts[0], chosen[0]),
        flops,
    )
    rows, token_sums = call(
        second_pack_kernel,
        "second_pack",
        (packed, array((4, token_count), F32)),
        (first_rows, own_sums, *parts[1], chosen[1]),
        flops,
    )
    arrived = lax.all_to_all(rows, "req", split_axis=0, concat_axis=0, tiled=True)

    token_sums = lax.psum(token_sums, "tp").reshape(2, 2, token_count)
    own_sums, next_sums = (
        jnp.sum(picks[None] * sums[:, None, :], axis=2) for picks, sums in zip(in_row, token_sums)
    )
    got = swap(next_sums, "req", 1)
    row_sums = (own_sums + got) / feature_total
    mean_value = row_sums[0]
    inverse = lax.rsqrt(row_sums[1] - mean_value * mean_value + 1e-05) * row_live
    stats = jnp.stack([inverse, -mean_value * inverse, row_live])
    stats = stats.reshape(3, 1, devices_req, capacity)
    got = swap(stats, "req", 1)
    lower = side == 0
    stats = jnp.concatenate(
        [jnp.where(lower, stats, got), jnp.where(lower, got, stats)], axis=1
    )
    stats = jnp.concatenate(
        [stats] + [swap(stats, "req", 2 * bits) for bits in range(1, planes)], axis=1
    )
    stats = lax.dynamic_index_in_dim(stats, me, 2, keepdims=False)
    stats = stats.reshape(3, devices_req * capacity)
    return finish(plane, stats, proj_gain, proj_bias, arrived)


def solution(mesh):
    placed = (
        P("req", None),
        P(),
        P("req", "tp"),
        P("tp"),
        P("tp"),
        P("tp", "req"),
        P("req", None),
        P("req"),
        P(None, "tp"),
        P(None, "tp"),
    )
    planes, odd = divmod(mesh.shape["req"], 2)
    fits = not odd and planes == mesh.shape["tp"] == 4
    return jax.shard_map(
        body if fits else general_body, mesh=mesh, in_specs=placed, out_specs=P("req", None, "tp"), check_vma=False
    )
```
